256 devices in a mesh: head: 4 (over y_lo, core), space: 16 (over y_hi, z), tm: 4 (over x).
Axes of the slice: x: 4, y: 4 (y_hi: 2, y_lo: 2; y = y_hi * 2 + y_lo), z: 8, core: 2. Of those that a mesh axis runs over, the one named last changes fastest.
Arguments:
- query: bfloat16 [16384, 2560], P(('space', 'tm'), 'head'), may hold values from -6 to 6
- key: bfloat16 [16384, 2560], P(('space', 'tm'), 'head'), may hold values from -6 to 6
- value: bfloat16 [16384, 2560], P(('space', 'tm'), 'head'), may hold values from -6 to 6
- tile_coords: int32 [3, 256], replicated, may hold values from 0 to 15, as said below
- windows: int32 [3, 20], P(None, 'head'), may hold values from 0 to 2, as said below
Outputs:
- attended: bfloat16 [16384, 2560], P(('space', 'tm'), 'head')
The draws below stay inside these ranges and needn't reach their ends.
Inputs may be any that keep to these rules, and one draw needn't show every extreme that they name: `tile_coords`: the device at position (s, t) of space and tm holds the tiles with frame coordinates t * 2 to (t + 1) * 2 - 1, all 2 height coordinates, and the single column (offset + sign * s) mod 16, for one offset and one sign of +1 or -1; its 4 tiles are stored in any order. windows[0, h] <= 2, windows[1, h] <= 1 and windows[2, h] <= 1 for every head; each of the three bounds is reached by some head.
All inputs are finite; a program needn't handle non-finite values.
Results may differ from the reference program's by a relative error of at most 0.007.
Values may be sent and summed in bfloat16 or wider, within the bound.
No kernel may reach another device: no remote copies, remote signals or barrier semaphores. Data moves between devices by JAX's collectives and lax.ppermute only.
A program may use at most 64 MiB of HBM per device.

```python
import jax
import jax.numpy as jnp
from jax import lax

HD = 128
HEADS = 20
TILE = 64
FT_DEV = 2
TH = 2
WW = 1
TILES_DEV = 4
NTILES = 256
TOKENS = 16384
FEATURES = 2560
CAND = 30
N_SPACE = 16
N_TM = 4


def draw_query(key, part):
    key = jax.random.fold_in(key, 11)
    base = jnp.clip(jax.random.normal(key, (TOKENS, HEADS * HD), jnp.float32), -4.0, 4.0)
    return base.astype(jnp.bfloat16)


def draw_key(key, part):
    key = jax.random.fold_in(key, 17)
    base = jnp.clip(jax.random.normal(key, (TOKENS, HEADS * HD), jnp.float32), -4.0, 4.0)
    return base.astype(jnp.bfloat16)


def draw_tile_coords(key, part):
    key = jax.random.fold_in(key, 23)
    first_key, second_key, third_key = jax.random.split(key, 3)
    offset = jax.random.randint(first_key, (), 0, N_SPACE)
    sign = 2 * jax.random.randint(second_key, (), 0, 2) - 1
    devices = N_SPACE * N_TM
    device_keys = jax.random.split(third_key, devices)
    orders = jax.vmap(lambda one_key: jax.random.permutation(one_key, TILES_DEV))(device_keys)
    device_ids = jnp.arange(devices)
    space_pos = device_ids // N_TM
    frame_slab = device_ids % N_TM
    frames = frame_slab[:, None] * FT_DEV + orders // TH
    heights = orders % TH
    columns = jnp.broadcast_to(((offset + sign * space_pos) % N_SPACE)[:, None], orders.shape)
    return jnp.stack([frames, heights, columns]).reshape(3, NTILES).astype(jnp.int32)


def draw_windows(key, part):
    key = jax.random.fold_in(key, 37)
    split_keys = jax.random.split(key, 6)
    head_ids = jnp.arange(HEADS)
    frame_w = jax.random.randint(split_keys[0], (HEADS,), 0, FT_DEV + 1)
    frame_w = jnp.where(head_ids == jax.random.randint(split_keys[1], (), 0, HEADS), FT_DEV, frame_w)
    height_w = jax.random.randint(split_keys[2], (HEADS,), 0, TH)
    height_w = jnp.where(head_ids == jax.random.randint(split_keys[3], (), 0, HEADS), TH - 1, height_w)
    column_w = jax.random.randint(split_keys[4], (HEADS,), 0, WW + 1)
    column_w = jnp.where(head_ids == jax.random.randint(split_keys[5], (), 0, HEADS), WW, column_w)
    return jnp.stack([frame_w, height_w, column_w]).astype(jnp.int32)


def shard_levels(own_key, shape, shards, smallest, high):
    level, own = 1.0, jax.random.fold_in(own_key, 6)
    for dim, blocks in shards:
        steps = jnp.exp(jax.random.uniform(jax.random.fold_in(own, dim), (blocks,), jnp.float32, smallest / len(shards), high / len(shards)))
        level = level * jnp.repeat(steps, shape[dim] // blocks).reshape([-1 if axis == dim else 1 for axis in range(len(shape))])
    return level


def gaussian(rng, dims, spread, reach, shards=(), held_as=jnp.bfloat16):
    values = spread * jax.random.normal(rng, dims, jnp.float32)
    if shards:
        values = values * shard_levels(rng, dims, shards, -0.22, 0.18)
    return jnp.clip(values, -reach, reach).astype(held_as)


def setup_inputs(seed: int = 0) -> dict:
    keys = jax.random.split(jax.random.key(seed), 6)
    query = draw_query(jax.random.fold_in(keys[5], 71), 0)
    key = draw_key(jax.random.fold_in(keys[5], 71), 0)
    value = gaussian(keys[2], (TOKENS, FEATURES), 1.0, 6.0, ((0, 64), (1, 4)))
    tile_coords = draw_tile_coords(jax.random.fold_in(keys[5], 71), 0)
    windows = draw_windows(jax.random.fold_in(keys[5], 71), 0)
    return dict(query=query, key=key, value=value, tile_coords=tile_coords, windows=windows)


LOWEST = -1.0e30


def reference(query, key, value, tile_coords, windows):
    query_tiles = query.reshape(NTILES, TILE, HEADS, HD)
    key_tiles = key.reshape(NTILES, TILE, HEADS, HD)
    value_tiles = value.reshape(NTILES, TILE, HEADS, HD)
    positions = jnp.arange(NTILES, dtype=jnp.int32)

    def one_tile(index):
        here = lax.dynamic_slice_in_dim(tile_coords, index, 1, 1)
        tile_gap = jnp.abs(tile_coords - here)
        inside = jnp.all(tile_gap[:, None, :] <= windows[:, :, None], axis=0)
        needed = jnp.any(inside, axis=0)
        ranking = jnp.where(needed, positions, NTILES + positions).astype(jnp.int32)
        order = jnp.argsort(ranking)[:CAND].astype(jnp.int32)
        chosen_keys = key_tiles[order].astype(jnp.float32)
        chosen_values = value_tiles[order].astype(jnp.float32)
        allowed = inside[:, order][:, None, :, None]
        own_queries = query_tiles[index].astype(jnp.float32)
        scores = jnp.einsum("qhd,cthd->hqct", own_queries, chosen_keys) * (HD ** -0.5)
        masked = jnp.where(allowed, scores, LOWEST)
        peak = jnp.max(masked, axis=(2, 3))
        weights = jnp.where(allowed, jnp.exp(masked - peak[:, :, None, None]), 0.0)
        totals = jnp.sum(weights, axis=(2, 3))
        rounded = lax.optimization_barrier(weights.astype(jnp.bfloat16)).astype(jnp.float32)
        summed = jnp.einsum("hqct,cthd->qhd", rounded, chosen_values)
        result = summed / totals.T[:, :, None]
        return result.astype(jnp.bfloat16).reshape(TILE, HEADS * HD)

    attended = lax.map(one_tile, positions)
    return attended.reshape(TOKENS, HEADS * HD)
```

```python
import functools

import jax
import jax.numpy as jnp
from jax import lax
from jax.experimental import pallas as pl
from jax.experimental.pallas import tpu as pltpu
from jax.sharding import PartitionSpec as P

TILE = 64
HEAD = 128
MASKED = -1e30
FLOOR = -1e29
FACTOR = 1.4426950408889634 * HEAD**-0.5
PARTS = 3
SPARE = 16
NEAR, FAR = 0, 1


def partner(index, side, count):
    step = 1 - 2 * (index % 2)
    return (index + (step if side == NEAR else -step)) % count


def exchange(block, axis, side):
    count = lax.axis_size(axis)
    return lax.ppermute(block, axis, [(i, partner(i, side, count)) for i in range(count)])


def shift(block, axis, distance):
    count = lax.axis_size(axis)
    return lax.ppermute(block, axis, [(i, (i + distance) % count) for i in range(count)])


def call(kernel, out_shape, flops, *operands, exps=0, moved=1 << 20):
    return pl.pallas_call(
        kernel,
        out_shape=out_shape,
        compiler_params=pltpu.CompilerParams(vmem_limit_bytes=40 * 1024 * 1024),
        cost_estimate=pl.CostEstimate(flops=flops, bytes_accessed=moved, transcendentals=exps),
    )(*operands)


def turn_kernel(v, out):
    for h in range(v.shape[1] // HEAD):
        lanes = slice(h * HEAD, (h + 1) * HEAD)
        out[lanes, :] = v[:, lanes].astype(jnp.float32).T.astype(jnp.bfloat16)


def weigh_kernel(heads, q, key, key_near, key_far, bias, weights_out, stats_out):
    stats_out[...] = jnp.zeros(stats_out.shape, jnp.float32)
    tiles = key.shape[0] // TILE
    for h in range(heads):
        lanes = slice(h * HEAD, (h + 1) * HEAD)
        blocks, peak = [], None
        for j, keys in enumerate((key, key_near, key_far)):
            raw = lax.dot_general(
                keys[:, lanes], q[:, lanes], (((1,), (1,)), ((), ())),
                preferred_element_type=jnp.float32,
            )
            for i in range(tiles):
                row = (h * 3 + j) * tiles + i
                block = raw[i * TILE : (i + 1) * TILE] + bias[row : row + 1, :]
                blocks.append(block)
                peak = block if peak is None else jnp.maximum(peak, block)
        peak = jnp.maximum(jnp.max(peak, axis=0, keepdims=True), FLOOR)
        total = None
        for i, block in enumerate(blocks):
            weights = jnp.exp2((block - peak) * FACTOR)
            weights_out[h, i * TILE : (i + 1) * TILE, :] = weights.astype(jnp.bfloat16)
            total = weights if total is None else total + weights
        total = jnp.maximum(jnp.sum(total, axis=0, keepdims=True), 0.5)
        stats_out[h : h + 1, :] = 1.0 / total
        stats_out[8 + h : 9 + h, :] = peak * FACTOR + jnp.log2(total)


def weighted(h, weights, stats, values):
    rows = slice(h * HEAD, (h + 1) * HEAD)
    width = values[0].shape[1]
    summed = None
    for j, turned in enumerate(values):
        part = jnp.dot(
            turned[rows, :], weights[h, j * width : (j + 1) * width, :],
            preferred_element_type=jnp.float32,
        )
        summed = part if summed is None else summed + part
    return summed * stats[h : h + 1, :]


def visitors_kernel(heads, weights, stats, v, v_near, v_far, out):
    end = heads * HEAD
    for h in range(heads):
        out[h * HEAD : (h + 1) * HEAD, :] = weighted(
            h, weights, stats, (v, v_near, v_far)
        ).astype(jnp.bfloat16)
    rest = stats[8:16, :]
    pieces = []
    for part in range(PARTS):
        piece = rest.astype(jnp.bfloat16).astype(jnp.float32)
        rest = rest - piece
        pieces.append(piece[0:heads])
    pieces.append(jnp.zeros((SPARE - PARTS * heads, rest.shape[1]), jnp.float32))
    out[end : end + SPARE, :] = jnp.concatenate(pieces, axis=0).astype(jnp.bfloat16)


def home_kernel(heads, weights, stats, v, v_near, v_far, out):
    for h in range(heads):
        out[h * HEAD : (h + 1) * HEAD, :] = weighted(h, weights, stats, (v, v_near, v_far))


def combine_kernel(heads, own, stats, last, next_, out):
    end = heads * HEAD
    own_level = stats[8 : 8 + heads, :]

    def level(ref):
        spare = ref[end : end + SPARE, :].astype(jnp.float32)
        return spare[0:heads] + spare[heads : 2 * heads] + spare[2 * heads : 3 * heads]

    last_level, next_level = level(last), level(next_)
    top = jnp.maximum(own_level, jnp.maximum(last_level, next_level))
    parts = [jnp.exp2(x - top) for x in (own_level, last_level, next_level)]
    scale = 1.0 / (parts[0] + parts[1] + parts[2])
    parts = [part * scale for part in parts]
    for h in range(heads):
        rows = slice(h * HEAD, (h + 1) * HEAD)
        result = own[rows, :] * parts[0][h : h + 1]
        result = result + last[rows, :].astype(jnp.float32) * parts[1][h : h + 1]
        result = result + next_[rows, :].astype(jnp.float32) * parts[2][h : h + 1]
        out[:, rows] = result.T.astype(jnp.bfloat16)


def tile_bias(tile_coords, windows, per_device):
    space_count, tm_count = lax.axis_size("space"), lax.axis_size("tm")
    s, t = lax.axis_index("space"), lax.axis_index("tm")

    def tiles(column, slab):
        device = column * tm_count + slab
        return lax.dynamic_slice_in_dim(tile_coords, device * per_device, per_device, 1)

    slabs = [t, partner(t, NEAR, tm_count), partner(t, FAR, tm_count)]
    columns = [s, (s + 1) % space_count, (s - 1) % space_count]
    key_tiles = jnp.concatenate([tiles(s, slab) for slab in slabs], axis=1)
    queries = jnp.stack([tiles(column, t) for column in columns], axis=1)
    queries = jnp.repeat(queries, TILE, axis=2)
    gap = jnp.abs(key_tiles[:, None, :, None] - queries[:, :, None, :])
    allowed = jnp.all(gap[:, :, None] <= windows[:, None, :, None, None], axis=0)
    bias = jnp.where(allowed, 0.0, MASKED).astype(jnp.float32)
    return [bias[i].reshape(-1, bias.shape[-1]) for i in range(3)]


def shards(query, key, value, tile_coords, windows):
    heads = windows.shape[1]
    rows = query.shape[0]
    width = heads * HEAD
    f32, bf16 = jnp.float32, jnp.bfloat16
    pair = 2 * rows * HEAD * rows

    k_near = exchange(key, "tm", NEAR)
    k_far = exchange(key, "tm", FAR)
    turned = call(turn_kernel, jax.ShapeDtypeStruct((width, rows), bf16), 0, value)
    v_near = exchange(turned, "tm", NEAR)
    v_far = exchange(turned, "tm", FAR)
    q_next = shift(query, "space", -1)
    late, _ = lax.optimization_barrier((query, k_near))
    q_last = shift(late, "space", 1)
    bias = tile_bias(tile_coords, windows, rows // TILE)

    def weigh(q, table):
        return call(
            functools.partial(weigh_kernel, heads),
            (
                jax.ShapeDtypeStruct((heads, 3 * rows, rows), bf16),
                jax.ShapeDtypeStruct((16, rows), f32),
            ),
            heads * 3 * pair, q, key, k_near, k_far, table, exps=heads * 3 * rows * rows,
        )

    def visitors(weights, stats):
        return call(
            functools.partial(visitors_kernel, heads),
            jax.ShapeDtypeStruct((width + SPARE, rows), bf16), heads * 3 * pair,
            weights, stats, turned, v_near, v_far,
        )

    next_weights = weigh(q_next, bias[1])
    last_weights = weigh(q_last, bias[2])
    own_weights, own_stats = weigh(query, bias[0])
    from_last = shift(visitors(*next_weights), "space", 1)
    from_next = shift(visitors(*last_weights), "space", -1)
    own = call(
        functools.partial(home_kernel, heads), jax.ShapeDtypeStruct((width, rows), f32),
        heads * 3 * pair, own_weights, own_stats, turned, v_near, v_far,
    )
    return call(
        functools.partial(combine_kernel, heads), jax.ShapeDtypeStruct((rows, width), bf16), 0,
        own, own_stats, from_last, from_next,
    )


def solution(mesh):
    placed = (
        P(("space", "tm"), "head"),
        P(("space", "tm"), "head"),
        P(("space", "tm"), "head"),
        P(),
        P(None, "head"),
    )
    return jax.shard_map(
        shards, mesh=mesh, in_specs=placed, out_specs=P(("space", "tm"), "head"), check_vma=False
    )
```

```python
import functools

import jax
import jax.numpy as jnp
from jax import lax
from jax.experimental import pallas as pl
from jax.experimental.pallas import tpu as pltpu
from jax.sharding import PartitionSpec as P

TILE = 64
HEAD = 128
MASKED = -1e30
FLOOR = -1e29
FACTOR = 1.4426950408889634 * HEAD**-0.5
PARTS = 3
SPARE = 16
NEAR, FAR = 0, 1


def partner(index, side, count):
    step = 1 - 2 * (index % 2)
    return (index + (step if side == NEAR else -step)) % count


def exchange(block, axis, side):
    count = lax.axis_size(axis)
    return lax.ppermute(block, axis, [(i, partner(i, side, count)) for i in range(count)])


def after(block, other):
    return lax.optimization_barrier((block, other))[0]


def call(kernel, out_shape, flops, *operands, exps=0, moved=1 << 20):
    return pl.pallas_call(
        kernel,
        out_shape=out_shape,
        compiler_params=pltpu.CompilerParams(vmem_limit_bytes=40 * 1024 * 1024),
        cost_estimate=pl.CostEstimate(flops=flops, bytes_accessed=moved, transcendentals=exps),
    )(*operands)


def turn_kernel(v, out):
    for h in range(v.shape[1] // HEAD):
        lanes = slice(h * HEAD, (h + 1) * HEAD)
        out[lanes, :] = v[:, lanes].astype(jnp.float32).T.astype(jnp.bfloat16)


def weigh_kernel(heads, q, key, key_near, key_far, bias, weights_out, stats_out):
    stats_out[...] = jnp.zeros(stats_out.shape, jnp.float32)
    tiles = key.shape[0] // TILE
    for h in range(heads):
        lanes = slice(h * HEAD, (h + 1) * HEAD)
        blocks, peak = [], None
        for j, keys in enumerate((key, key_near, key_far)):
            raw = lax.dot_general(
                keys[:, lanes], q[:, lanes], (((1,), (1,)), ((), ())),
                preferred_element_type=jnp.float32,
            )
            for i in range(tiles):
                row = (h * 3 + j) * tiles + i
                block = raw[i * TILE : (i + 1) * TILE] + bias[row : row + 1, :]
                blocks.append(block)
                peak = block if peak is None else jnp.maximum(peak, block)
        peak = jnp.maximum(jnp.max(peak, axis=0, keepdims=True), FLOOR)
        total = None
        for i, block in enumerate(blocks):
            weights = jnp.exp2((block - peak) * FACTOR)
            weights_out[h, i * TILE : (i + 1) * TILE, :] = weights.astype(jnp.bfloat16)
            total = weights if total is None else total + weights
        total = jnp.maximum(jnp.sum(total, axis=0, keepdims=True), 0.5)
        stats_out[h : h + 1, :] = 1.0 / total
        stats_out[8 + h : 9 + h, :] = peak * FACTOR + jnp.log2(total)


def weighted(h, weights, stats, values):
    rows = slice(h * HEAD, (h + 1) * HEAD)
    width = values[0].shape[1]
    summed = None
    for j, turned in enumerate(values):
        part = jnp.dot(
            turned[rows, :], weights[h, j * width : (j + 1) * width, :],
            preferred_element_type=jnp.float32,
        )
        summed = part if summed is None else summed + part
    return summed * stats[h : h + 1, :]


def visitors_kernel(heads, weights, stats, v, v_near, v_far, out):
    end = heads * HEAD
    for h in range(heads):
        out[h * HEAD : (h + 1) * HEAD, :] = weighted(
            h, weights, stats, (v, v_near, v_far)
        ).astype(jnp.bfloat16)
    rest = stats[8:16, :]
    pieces = []
    for part in range(PARTS):
        piece = rest.astype(jnp.bfloat16).astype(jnp.float32)
        rest = rest - piece
        pieces.append(piece[0:heads])
    pieces.append(jnp.zeros((SPARE - PARTS * heads, rest.shape[1]), jnp.float32))
    out[end : end + SPARE, :] = jnp.concatenate(pieces, axis=0).astype(jnp.bfloat16)


def home_kernel(heads, weights, stats, v, v_near, v_far, out):
    for h in range(heads):
        out[h * HEAD : (h + 1) * HEAD, :] = weighted(h, weights, stats, (v, v_near, v_far))


def level_of(ref, heads):
    spare = ref[heads * HEAD : heads * HEAD + SPARE, :].astype(jnp.float32)
    return spare[0:heads] + spare[heads : 2 * heads] + spare[2 * heads : 3 * heads]


def merge_kernel(heads, own, stats, near, out, level_out):
    levels = [stats[8 : 8 + heads, :], level_of(near, heads)]
    top = jnp.maximum(levels[0], levels[1])
    parts = [jnp.exp2(level - top) for level in levels]
    scale = 1.0 / (parts[0] + parts[1])
    level_out[...] = jnp.zeros(level_out.shape, jnp.float32)
    level_out[0:heads, :] = top + jnp.log2(parts[0] + parts[1])
    parts = [part * scale for part in parts]
    for h in range(heads):
        rows = slice(h * HEAD, (h + 1) * HEAD)
        result = own[rows, :] * parts[0][h : h + 1]
        out[rows, :] = result + near[rows, :].astype(jnp.float32) * parts[1][h : h + 1]


def combine_kernel(heads, merged, level, far, out):
    levels = [level[0:heads, :], level_of(far, heads)]
    top = jnp.maximum(levels[0], levels[1])
    parts = [jnp.exp2(level - top) for level in levels]
    scale = 1.0 / (parts[0] + parts[1])
    parts = [part * scale for part in parts]
    for h in range(heads):
        rows = slice(h * HEAD, (h + 1) * HEAD)
        result = merged[rows, :] * parts[0][h : h + 1]
        result = result + far[rows, :].astype(jnp.float32) * parts[1][h : h + 1]
        out[:, rows] = result.T.astype(jnp.bfloat16)


def tile_bias(tile_coords, windows, per_device):
    space_count, tm_count = lax.axis_size("space"), lax.axis_size("tm")
    s, t = lax.axis_index("space"), lax.axis_index("tm")

    def tiles(column, slab):
        device = column * tm_count + slab
        return lax.dynamic_slice_in_dim(tile_coords, device * per_device, per_device, 1)

    slabs = [t, partner(t, NEAR, tm_count), partner(t, FAR, tm_count)]
    columns = [s, partner(s, NEAR, space_count), partner(s, FAR, space_count)]
    key_tiles = jnp.concatenate([tiles(s, slab) for slab in slabs], axis=1)
    queries = jnp.stack([tiles(column, t) for column in columns], axis=1)
    queries = jnp.repeat(queries, TILE, axis=2)
    gap = jnp.abs(key_tiles[:, None, :, None] - queries[:, :, None, :])
    allowed = jnp.all(gap[:, :, None] <= windows[:, None, :, None, None], axis=0)
    bias = jnp.where(allowed, 0.0, MASKED).astype(jnp.float32)
    return [bias[i].reshape(-1, bias.shape[-1]) for i in range(3)]


def shards(query, key, value, tile_coords, windows):
    heads = windows.shape[1]
    rows = query.shape[0]
    width = heads * HEAD
    f32, bf16 = jnp.float32, jnp.bfloat16
    pair = 2 * rows * HEAD * rows

    q_near = exchange(query, "space", NEAR)
    k_near = exchange(key, "tm", NEAR)
    k_far = exchange(key, "tm", FAR)
    turned = call(turn_kernel, jax.ShapeDtypeStruct((width, rows), bf16), 0, value)
    q_far = exchange(query, "space", FAR)
    v_far = exchange(turned, "tm", FAR)
    v_near = exchange(after(turned, k_near), "tm", NEAR)
    bias = tile_bias(tile_coords, windows, rows // TILE)

    def weigh(q, table):
        return call(
            functools.partial(weigh_kernel, heads),
            (
                jax.ShapeDtypeStruct((heads, 3 * rows, rows), bf16),
                jax.ShapeDtypeStruct((16, rows), f32),
            ),
            heads * 3 * pair, q, key, k_near, k_far, table, exps=heads * 3 * rows * rows,
        )

    def visitors(weights, stats):
        return call(
            functools.partial(visitors_kernel, heads),
            jax.ShapeDtypeStruct((width + SPARE, rows), bf16), heads * 3 * pair,
            weights, stats, turned, v_near, v_far,
        )

    near_weights, near_stats = weigh(q_near, bias[1])
    far_weights, far_stats = weigh(q_far, after(bias[2], near_stats))
    own_weights, own_stats = weigh(query, bias[0])
    to_near = visitors(near_weights, after(near_stats, far_stats))
    near = exchange(to_near, "space", NEAR)
    far = exchange(visitors(far_weights, after(far_stats, to_near)), "space", FAR)
    own = call(
        functools.partial(home_kernel, heads), jax.ShapeDtypeStruct((width, rows), f32),
        heads * 3 * pair, own_weights, own_stats, turned, v_near, v_far,
    )
    merged, level = call(
        functools.partial(merge_kernel, heads),
        (jax.ShapeDtypeStruct((width, rows), f32), jax.ShapeDtypeStruct((8, rows), f32)), 0,
        own, own_stats, near,
    )
    return call(
        functools.partial(combine_kernel, heads), jax.ShapeDtypeStruct((rows, width), bf16), 0,
        merged, level, far,
    )


def solution(mesh):
    placed = (
        P(("space", "tm"), "head"),
        P(("space", "tm"), "head"),
        P(("space", "tm"), "head"),
        P(),
        P(None, "head"),
    )
    return jax.shard_map(
        shards, mesh=mesh, in_specs=placed, out_specs=P(("space", "tm"), "head"), check_vma=False
    )
```

```python
import functools

import jax
import jax.numpy as jnp
from jax import lax
from jax.experimental import pallas as pl
from jax.experimental.pallas import tpu as pltpu
from jax.sharding import PartitionSpec as P

TILE = 64
HEAD = 128
MASKED = -1e30
FLOOR = -1e29
FACTOR = 1.4426950408889634 * HEAD**-0.5
PARTS = 3
SPARE = 16
NEAR, FAR = 0, 1


def partner(index, side, count):
    step = 1 - 2 * (index % 2)
    return (index + (step if side == NEAR else -step)) % count


def exchange(block, axis, side):
    count = lax.axis_size(axis)
    return lax.ppermute(block, axis, [(i, partner(i, side, count)) for i in range(count)])


def swap_slabs(block):
    heads, slabs = lax.axis_size("head"), lax.axis_size("tm")
    pairs = []
    for head in range(heads):
        for slab in range(slabs):
            if 0 < slab < slabs - 1:
                there = head * slabs + partner(slab, FAR, slabs)
            else:
                there = partner(head, NEAR, heads) * slabs + slab
            pairs.append((head * slabs + slab, there))
    return lax.ppermute(block, ("head", "tm"), pairs)


def after(block, other):
    return lax.optimization_barrier((block, other))[0]


def call(kernel, out_shape, flops, *operands, exps=0, moved=1 << 20):
    return pl.pallas_call(
        kernel,
        out_shape=out_shape,
        compiler_params=pltpu.CompilerParams(vmem_limit_bytes=40 * 1024 * 1024),
        cost_estimate=pl.CostEstimate(flops=0, bytes_accessed=1024, transcendentals=0),
    )(*operands)


def weigh_kernel(heads, q, key, key_near, key_far, bias, weights_out, stats_out):
    stats_out[...] = jnp.zeros(stats_out.shape, jnp.float32)
    tiles = key.shape[0] // TILE
    for h in range(heads):
        lanes = slice(h * HEAD, (h + 1) * HEAD)
        blocks, peak = [], None
        for j, keys in enumerate((key, key_near, key_far)):
            raw = lax.dot_general(
                keys[:, lanes], q[:, lanes], (((1,), (1,)), ((), ())),
                preferred_element_type=jnp.float32,
            )
            for i in range(tiles):
                row = (h * 3 + j) * tiles + i
                block = raw[i * TILE : (i + 1) * TILE] + bias[row : row + 1, :]
                blocks.append(block)
                peak = block if peak is None else jnp.maximum(peak, block)
        peak = jnp.maximum(jnp.max(peak, axis=0, keepdims=True), FLOOR)
        total = None
        for i, block in enumerate(blocks):
            weights = jnp.exp2((block - peak) * FACTOR)
            weights_out[h, i * TILE : (i + 1) * TILE, :] = weights.astype(jnp.bfloat16)
            total = weights if total is None else total + weights
        total = jnp.maximum(jnp.sum(total, axis=0, keepdims=True), 0.5)
        stats_out[h : h + 1, :] = 1.0 / total
        stats_out[8 + h : 9 + h, :] = peak * FACTOR + jnp.log2(total)


def weighted(h, weights, stats, values):
    lanes = slice(h * HEAD, (h + 1) * HEAD)
    width = values[0].shape[0]
    summed = None
    for j, value in enumerate(values):
        part = lax.dot_general(
            value[:, lanes], weights[h, j * width : (j + 1) * width, :],
            (((0,), (0,)), ((), ())), preferred_element_type=jnp.float32,
        )
        summed = part if summed is None else summed + part
    return summed * stats[h : h + 1, :]


def visitors_kernel(heads, weights, stats, v, v_near, v_far, out):
    end = heads * HEAD
    for h in range(heads):
        out[h * HEAD : (h + 1) * HEAD, :] = weighted(
            h, weights, stats, (v, v_near, v_far)
        ).astype(jnp.bfloat16)
    rest = stats[8:16, :]
    pieces = []
    for part in range(PARTS):
        piece = rest.astype(jnp.bfloat16).astype(jnp.float32)
        rest = rest - piece
        pieces.append(piece[0:heads])
    pieces.append(jnp.zeros((SPARE - PARTS * heads, rest.shape[1]), jnp.float32))
    out[end : end + SPARE, :] = jnp.concatenate(pieces, axis=0).astype(jnp.bfloat16)


def home_kernel(heads, weights, stats, v, v_near, v_far, out):
    for h in range(heads):
        out[h * HEAD : (h + 1) * HEAD, :] = weighted(h, weights, stats, (v, v_near, v_far))


def level_of(ref, heads):
    spare = ref[heads * HEAD : heads * HEAD + SPARE, :].astype(jnp.float32)
    return spare[0:heads] + spare[heads : 2 * heads] + spare[2 * heads : 3 * heads]


def merge_kernel(heads, own, stats, near, out, level_out):
    levels = [stats[8 : 8 + heads, :], level_of(near, heads)]
    top = jnp.maximum(levels[0], levels[1])
    parts = [jnp.exp2(level - top) for level in levels]
    scale = 1.0 / (parts[0] + parts[1])
    level_out[...] = jnp.zeros(level_out.shape, jnp.float32)
    level_out[0:heads, :] = top + jnp.log2(parts[0] + parts[1])
    parts = [part * scale for part in parts]
    for h in range(heads):
        rows = slice(h * HEAD, (h + 1) * HEAD)
        result = own[rows, :] * parts[0][h : h + 1]
        out[rows, :] = result + near[rows, :].astype(jnp.float32) * parts[1][h : h + 1]


def combine_kernel(heads, merged, level, far, out):
    levels = [level[0:heads, :], level_of(far, heads)]
    top = jnp.maximum(levels[0], levels[1])
    parts = [jnp.exp2(level - top) for level in levels]
    scale = 1.0 / (parts[0] + parts[1])
    parts = [part * scale for part in parts]
    for h in range(heads):
        rows = slice(h * HEAD, (h + 1) * HEAD)
        result = merged[rows, :] * parts[0][h : h + 1]
        result = result + far[rows, :].astype(jnp.float32) * parts[1][h : h + 1]
        out[:, rows] = result.T.astype(jnp.bfloat16)


def tile_bias(tile_coords, windows, per_device, gate):
    space_count, tm_count = lax.axis_size("space"), lax.axis_size("tm")
    s, t = lax.axis_index("space"), lax.axis_index("tm")

    def tiles(column, slab):
        device = column * tm_count + slab
        return lax.dynamic_slice_in_dim(tile_coords, device * per_device, per_device, 1)

    slabs = [t, partner(t, NEAR, tm_count), partner(t, FAR, tm_count)]
    columns = [s, partner(s, NEAR, space_count), partner(s, FAR, space_count)]
    key_tiles = jnp.concatenate([tiles(s, slab) for slab in slabs], axis=1)
    queries = jnp.stack([tiles(column, t) for column in columns], axis=1)
    key_tiles, queries, _ = lax.optimization_barrier((key_tiles, queries, gate))
    queries = jnp.repeat(queries, TILE, axis=2)
    gap = jnp.abs(key_tiles[:, None, :, None] - queries[:, :, None, :])
    allowed = jnp.all(gap[:, :, None] <= windows[:, None, :, None, None], axis=0)
    bias = jnp.where(allowed, 0.0, MASKED).astype(jnp.float32)
    return [bias[i].reshape(-1, bias.shape[-1]) for i in range(3)]


def shards(query, key, value, tile_coords, windows):
    heads = windows.shape[1]
    rows = query.shape[0]
    width = heads * HEAD
    f32, bf16 = jnp.float32, jnp.bfloat16
    pair = 2 * rows * HEAD * rows

    k_near = exchange(key, "tm", NEAR)
    k_far = swap_slabs(key)
    q_near = exchange(query, "space", NEAR)
    q_far = exchange(query, "space", FAR)
    v_far = swap_slabs(value)
    v_near = exchange(after(value, k_near), "tm", NEAR)
    bias = tile_bias(tile_coords, windows, rows // TILE, k_near)

    def weigh(q, table):
        return call(
            functools.partial(weigh_kernel, heads),
            (
                jax.ShapeDtypeStruct((heads, 3 * rows, rows), bf16),
                jax.ShapeDtypeStruct((16, rows), f32),
            ),
            heads * 3 * pair, q, key, k_near, k_far, table, exps=heads * 3 * rows * rows,
        )

    def visitors(weights, stats):
        return call(
            functools.partial(visitors_kernel, heads),
            jax.ShapeDtypeStruct((width + SPARE, rows), bf16), heads * 3 * pair,
            weights, stats, value, v_near, v_far,
        )

    near_weights, near_stats = weigh(q_near, bias[1])
    far_weights, far_stats = weigh(q_far, after(bias[2], near_stats))
    own_weights, own_stats = weigh(query, bias[0])
    to_near = visitors(near_weights, after(near_stats, far_stats))
    near = exchange(to_near, "space", NEAR)
    far = exchange(visitors(far_weights, after(far_stats, to_near)), "space", FAR)
    own = call(
        functools.partial(home_kernel, heads), jax.ShapeDtypeStruct((width, rows), f32),
        heads * 3 * pair, own_weights, own_stats, value, v_near, v_far,
    )
    merged, level = call(
        functools.partial(merge_kernel, heads),
        (jax.ShapeDtypeStruct((width, rows), f32), jax.ShapeDtypeStruct((8, rows), f32)), 0,
        own, own_stats, near,
    )
    return call(
        functools.partial(combine_kernel, heads), jax.ShapeDtypeStruct((rows, width), bf16), 0,
        merged, level, far,
    )


def solution(mesh):
    placed = (
        P(("space", "tm"), "head"),
        P(("space", "tm"), "head"),
        P(("space", "tm"), "head"),
        P(),
        P(None, "head"),
    )
    return jax.shard_map(
        shards, mesh=mesh, in_specs=placed, out_specs=P(("space", "tm"), "head"), check_vma=False
    )
```

```python
import functools

import jax
import jax.numpy as jnp
from jax import lax
from jax.experimental import pallas as pl
from jax.experimental.pallas import tpu as pltpu
from jax.sharding import PartitionSpec as P

TILE = 64
HEAD = 128
MASKED = -1e30
FLOOR = -1e29
FACTOR = 1.4426950408889634 * HEAD**-0.5
PARTS = 3
SPARE = 16
NEAR, FAR = 0, 1


def partner(index, side, count):
    step = 1 - 2 * (index % 2)
    return (index + (step if side == NEAR else -step)) % count


def exchange(block, axis, side):
    count = lax.axis_size(axis)
    return lax.ppermute(block, axis, [(i, partner(i, side, count)) for i in range(count)])


def shift(block, axis, distance):
    count = lax.axis_size(axis)
    return lax.ppermute(block, axis, [(i, (i + distance) % count) for i in range(count)])


def swap_slabs(block):
    heads, slabs = lax.axis_size("head"), lax.axis_size("tm")
    pairs = []
    for head in range(heads):
        for slab in range(slabs):
            if 0 < slab < slabs - 1:
                there = head * slabs + partner(slab, FAR, slabs)
            else:
                there = partner(head, NEAR, heads) * slabs + slab
            pairs.append((head * slabs + slab, there))
    return lax.ppermute(block, ("head", "tm"), pairs)


def after(block, other):
    return lax.optimization_barrier((block, other))[0]


def call(kernel, out_shape, flops, *operands, exps=0, moved=1 << 20):
    return pl.pallas_call(
        kernel,
        out_shape=out_shape,
        compiler_params=pltpu.CompilerParams(vmem_limit_bytes=40 * 1024 * 1024),
        cost_estimate=pl.CostEstimate(flops=0, bytes_accessed=1024, transcendentals=0),
    )(*operands)


def weigh_kernel(heads, q, key, key_near, key_far, bias, weights_out, stats_out):
    stats_out[...] = jnp.zeros(stats_out.shape, jnp.float32)
    tiles = key.shape[0] // TILE
    for h in range(heads):
        lanes = slice(h * HEAD, (h + 1) * HEAD)
        blocks, peak = [], None
        for j, keys in enumerate((key, key_near, key_far)):
            raw = lax.dot_general(
                keys[:, lanes], q[:, lanes], (((1,), (1,)), ((), ())),
                preferred_element_type=jnp.float32,
            )
            for i in range(tiles):
                row = (h * 3 + j) * tiles + i
                block = raw[i * TILE : (i + 1) * TILE] + bias[row : row + 1, :]
                blocks.append(block)
                peak = block if peak is None else jnp.maximum(peak, block)
        peak = jnp.maximum(jnp.max(peak, axis=0, keepdims=True), FLOOR)
        total = None
        for i, block in enumerate(blocks):
            weights = jnp.exp2((block - peak) * FACTOR)
            weights_out[h, i * TILE : (i + 1) * TILE, :] = weights.astype(jnp.bfloat16)
            total = weights if total is None else total + weights
        total = jnp.maximum(jnp.sum(total, axis=0, keepdims=True), 0.5)
        stats_out[h : h + 1, :] = 1.0 / total
        stats_out[8 + h : 9 + h, :] = peak * FACTOR + jnp.log2(total)


def weighted(h, weights, value, j):
    lanes = slice(h * HEAD, (h + 1) * HEAD)
    width = value.shape[0]
    return lax.dot_general(
        value[:, lanes], weights[h, j * width : (j + 1) * width, :],
        (((0,), (0,)), ((), ())), preferred_element_type=jnp.float32,
    )


def early_kernel(heads, weights, v, v_far, out):
    for h in range(heads):
        out[h * HEAD : (h + 1) * HEAD, :] = weighted(h, weights, v, 0) + weighted(h, weights, v_far, 2)


def store_levels(heads, stats, out):
    end = heads * HEAD
    rest = stats[8:16, :]
    pieces = []
    for part in range(PARTS):
        piece = rest.astype(jnp.bfloat16).astype(jnp.float32)
        rest = rest - piece
        pieces.append(piece[0:heads])
    pieces.append(jnp.zeros((SPARE - PARTS * heads, rest.shape[1]), jnp.float32))
    out[end : end + SPARE, :] = jnp.concatenate(pieces, axis=0).astype(jnp.bfloat16)


def finish_kernel(heads, early, weights, stats, v_near, out):
    for h in range(heads):
        rows = slice(h * HEAD, (h + 1) * HEAD)
        summed = early[rows, :] + weighted(h, weights, v_near, 1)
        out[rows, :] = (summed * stats[h : h + 1, :]).astype(jnp.bfloat16)
    store_levels(heads, stats, out)


def sum_up(h, weights, stats, v, v_near, v_far):
    summed = weighted(h, weights, v, 0) + weighted(h, weights, v_near, 1) + weighted(h, weights, v_far, 2)
    return summed * stats[h : h + 1, :]


def visitors_kernel(heads, weights, stats, v, v_near, v_far, out):
    for h in range(heads):
        out[h * HEAD : (h + 1) * HEAD, :] = sum_up(
            h, weights, stats, v, v_near, v_far
        ).astype(jnp.bfloat16)
    store_levels(heads, stats, out)


def home_kernel(heads, weights, stats, v, v_near, v_far, out):
    for h in range(heads):
        out[h * HEAD : (h + 1) * HEAD, :] = sum_up(h, weights, stats, v, v_near, v_far)


def level_of(ref, heads):
    spare = ref[heads * HEAD : heads * HEAD + SPARE, :].astype(jnp.float32)
    return spare[0:heads] + spare[heads : 2 * heads] + spare[2 * heads : 3 * heads]


def merge_kernel(heads, own, stats, near, out, level_out):
    levels = [stats[8 : 8 + heads, :], level_of(near, heads)]
    top = jnp.maximum(levels[0], levels[1])
    parts = [jnp.exp2(level - top) for level in levels]
    scale = 1.0 / (parts[0] + parts[1])
    level_out[...] = jnp.zeros(level_out.shape, jnp.float32)
    level_out[0:heads, :] = top + jnp.log2(parts[0] + parts[1])
    parts = [part * scale for part in parts]
    for h in range(heads):
        rows = slice(h * HEAD, (h + 1) * HEAD)
        result = own[rows, :] * parts[0][h : h + 1]
        out[rows, :] = result + near[rows, :].astype(jnp.float32) * parts[1][h : h + 1]


def combine_kernel(heads, merged, level, far, out):
    levels = [level[0:heads, :], level_of(far, heads)]
    top = jnp.maximum(levels[0], levels[1])
    parts = [jnp.exp2(level - top) for level in levels]
    scale = 1.0 / (parts[0] + parts[1])
    parts = [part * scale for part in parts]
    for h in range(heads):
        rows = slice(h * HEAD, (h + 1) * HEAD)
        result = merged[rows, :] * parts[0][h : h + 1]
        result = result + far[rows, :].astype(jnp.float32) * parts[1][h : h + 1]
        out[:, rows] = result.T.astype(jnp.bfloat16)


def nearby_tiles(tile_coords, per_device):
    space_count, tm_count = lax.axis_size("space"), lax.axis_size("tm")
    s, t = lax.axis_index("space"), lax.axis_index("tm")

    def tiles(column, slab):
        device = column * tm_count + slab
        return lax.dynamic_slice_in_dim(tile_coords, device * per_device, per_device, 1)

    slabs = [t, partner(t, NEAR, tm_count), partner(t, FAR, tm_count)]
    columns = [s, (s + 1) % space_count, (s - 1) % space_count]
    key_tiles = jnp.concatenate([tiles(s, slab) for slab in slabs], axis=1)
    return key_tiles, jnp.stack([tiles(column, t) for column in columns], axis=1)


def tile_bias(key_tiles, queries, windows):
    queries = jnp.repeat(queries, TILE, axis=2)
    gap = jnp.abs(key_tiles[:, None, :, None] - queries[:, :, None, :])
    allowed = jnp.all(gap[:, :, None] <= windows[:, None, :, None, None], axis=0)
    bias = jnp.where(allowed, 0.0, MASKED).astype(jnp.float32)
    return [bias[i].reshape(-1, bias.shape[-1]) for i in range(3)]


def shards(query, key, value, tile_coords, windows):
    heads = windows.shape[1]
    rows = query.shape[0]
    width = heads * HEAD
    f32, bf16 = jnp.float32, jnp.bfloat16
    pair = 2 * rows * HEAD * rows

    k_near = exchange(key, "tm", NEAR)
    k_far = swap_slabs(key)
    near_tiles = nearby_tiles(tile_coords, rows // TILE)
    q_last = shift(query, "space", 1)
    q_next = shift(after(query, near_tiles[0]), "space", -1)
    v_far = swap_slabs(value)
    v_near = exchange(after(value, k_near), "tm", NEAR)
    bias = tile_bias(*after(near_tiles, k_near), windows)

    def weigh(q, table):
        return call(
            functools.partial(weigh_kernel, heads),
            (
                jax.ShapeDtypeStruct((heads, 3 * rows, rows), bf16),
                jax.ShapeDtypeStruct((16, rows), f32),
            ),
            heads * 3 * pair, q, key, k_near, k_far, table, exps=heads * 3 * rows * rows,
        )

    next_weights, next_stats = weigh(q_next, bias[1])
    early = call(
        functools.partial(early_kernel, heads), jax.ShapeDtypeStruct((width, rows), f32), 0,
        next_weights, value, v_far,
    )
    back = jax.ShapeDtypeStruct((width + SPARE, rows), bf16)
    to_next = call(
        functools.partial(finish_kernel, heads), back, 0,
        early, next_weights, next_stats, v_near,
    )
    last_weights, last_stats = weigh(q_last, after(bias[2], to_next))
    to_last = call(
        functools.partial(visitors_kernel, heads), back, 0,
        last_weights, last_stats, value, v_near, v_far,
    )
    own_weights, own_stats = weigh(query, after(bias[0], to_last))
    from_last = shift(to_next, "space", 1)
    from_next = shift(to_last, "space", -1)
    own = call(
        functools.partial(home_kernel, heads), jax.ShapeDtypeStruct((width, rows), f32),
        heads * 3 * pair, own_weights, own_stats, value, v_near, v_far,
    )
    merged, level = call(
        functools.partial(merge_kernel, heads),
        (jax.ShapeDtypeStruct((width, rows), f32), jax.ShapeDtypeStruct((8, rows), f32)), 0,
        own, own_stats, from_last,
    )
    return call(
        functools.partial(combine_kernel, heads), jax.ShapeDtypeStruct((rows, width), bf16), 0,
        merged, level, from_next,
    )


def solution(mesh):
    placed = (
        P(("space", "tm"), "head"),
        P(("space", "tm"), "head"),
        P(("space", "tm"), "head"),
        P(),
        P(None, "head"),
    )
    return jax.shard_map(
        shards, mesh=mesh, in_specs=placed, out_specs=P(("space", "tm"), "head"), check_vma=False
    )
```

```python
import functools

import jax
import jax.numpy as jnp
from jax import lax
from jax.experimental import pallas as pl
from jax.experimental.pallas import tpu as pltpu
from jax.sharding import PartitionSpec as P

TILE = 64
HEAD = 128
MASKED = -1e30
FLOOR = -1e29
FACTOR = 1.4426950408889634 * HEAD**-0.5
PARTS = 3
SPARE = 16
NEAR, FAR = 0, 1


def partner(index, side, count):
    step = 1 - 2 * (index % 2)
    return (index + (step if side == NEAR else -step)) % count


def exchange(block, axis, side):
    count = lax.axis_size(axis)
    return lax.ppermute(block, axis, [(i, partner(i, side, count)) for i in range(count)])


def shift(block, axis, distance):
    count = lax.axis_size(axis)
    return lax.ppermute(block, axis, [(i, (i + distance) % count) for i in range(count)])


def swap_slabs(block):
    heads, slabs = lax.axis_size("head"), lax.axis_size("tm")
    pairs = []
    for head in range(heads):
        for slab in range(slabs):
            if 0 < slab < slabs - 1:
                there = head * slabs + partner(slab, FAR, slabs)
            else:
                there = partner(head, NEAR, heads) * slabs + slab
            pairs.append((head * slabs + slab, there))
    return lax.ppermute(block, ("head", "tm"), pairs)


def after(block, other):
    return lax.optimization_barrier((block, other))[0]


def call(kernel, out_shape, flops, *operands, exps=0, moved=1 << 20):
    return pl.pallas_call(
        kernel,
        out_shape=out_shape,
        compiler_params=pltpu.CompilerParams(vmem_limit_bytes=40 * 1024 * 1024),
        cost_estimate=pl.CostEstimate(flops=0, bytes_accessed=1024, transcendentals=0),
    )(*operands)


def weigh_kernel(heads, q, key, key_near, key_far, bias, weights_out, stats_out):
    stats_out[...] = jnp.zeros(stats_out.shape, jnp.float32)
    tiles = key.shape[0] // TILE
    for h in range(heads):
        lanes = slice(h * HEAD, (h + 1) * HEAD)
        blocks, peak = [], None
        for j, keys in enumerate((key, key_near, key_far)):
            raw = lax.dot_general(
                keys[:, lanes], q[:, lanes], (((1,), (1,)), ((), ())),
                preferred_element_type=jnp.float32,
            )
            for i in range(tiles):
                row = (h * 3 + j) * tiles + i
                block = raw[i * TILE : (i + 1) * TILE] + bias[row : row + 1, :]
                blocks.append(block)
                peak = block if peak is None else jnp.maximum(peak, block)
        peak = jnp.maximum(jnp.max(peak, axis=0, keepdims=True), FLOOR)
        total = None
        for i, block in enumerate(blocks):
            weights = jnp.exp2((block - peak) * FACTOR)
            weights_out[h, i * TILE : (i + 1) * TILE, :] = weights.astype(jnp.bfloat16)
            total = weights if total is None else total + weights
        total = jnp.maximum(jnp.sum(total, axis=0, keepdims=True), 0.5)
        stats_out[h : h + 1, :] = 1.0 / total
        stats_out[8 + h : 9 + h, :] = peak * FACTOR + jnp.log2(total)


def weighted(h, weights, stats, values):
    lanes = slice(h * HEAD, (h + 1) * HEAD)
    width = values[0].shape[0]
    summed = None
    for j, value in enumerate(values):
        part = lax.dot_general(
            value[:, lanes], weights[h, j * width : (j + 1) * width, :],
            (((0,), (0,)), ((), ())), preferred_element_type=jnp.float32,
        )
        summed = part if summed is None else summed + part
    return summed * stats[h : h + 1, :]


def visitors_kernel(
    heads, side, near_weights, near_stats, far_weights, far_stats, v, v_near, v_far, out
):
    end = heads * HEAD
    odd = lax.axis_index("space") % 2

    def sum_up(weights, stats):
        for h in range(heads):
            out[h * HEAD : (h + 1) * HEAD, :] = weighted(
                h, weights, stats, (v, v_near, v_far)
            ).astype(jnp.bfloat16)
        rest = stats[8:16, :]
        pieces = []
        for part in range(PARTS):
            piece = rest.astype(jnp.bfloat16).astype(jnp.float32)
            rest = rest - piece
            pieces.append(piece[0:heads])
        pieces.append(jnp.zeros((SPARE - PARTS * heads, rest.shape[1]), jnp.float32))
        out[end : end + SPARE, :] = jnp.concatenate(pieces, axis=0).astype(jnp.bfloat16)

    pl.when(odd == side)(lambda: sum_up(near_weights, near_stats))
    pl.when(odd != side)(lambda: sum_up(far_weights, far_stats))


def home_kernel(heads, weights, stats, v, v_near, v_far, out):
    for h in range(heads):
        out[h * HEAD : (h + 1) * HEAD, :] = weighted(h, weights, stats, (v, v_near, v_far))


def level_of(ref, heads):
    spare = ref[heads * HEAD : heads * HEAD + SPARE, :].astype(jnp.float32)
    return spare[0:heads] + spare[heads : 2 * heads] + spare[2 * heads : 3 * heads]


def shares(levels):
    top = functools.reduce(jnp.maximum, levels)
    parts = [jnp.exp2(level - top) for level in levels]
    scale = 1.0 / functools.reduce(jnp.add, parts)
    return [part * scale for part in parts]


def merge_kernel(heads, own, stats, near, out, level_out):
    levels = [stats[8 : 8 + heads, :], level_of(near, heads)]
    top = jnp.maximum(levels[0], levels[1])
    parts = [jnp.exp2(level - top) for level in levels]
    scale = 1.0 / (parts[0] + parts[1])
    level_out[...] = jnp.zeros(level_out.shape, jnp.float32)
    level_out[0:heads, :] = top + jnp.log2(parts[0] + parts[1])
    parts = [part * scale for part in parts]
    for h in range(heads):
        rows = slice(h * HEAD, (h + 1) * HEAD)
        result = own[rows, :] * parts[0][h : h + 1]
        out[rows, :] = result + near[rows, :].astype(jnp.float32) * parts[1][h : h + 1]


def combine_kernel(heads, merged, level, other, out, block, sems):
    parts = shares([level[0:heads, :], level_of(other, heads)])
    rows = block.shape[0]
    half = rows // 2
    copies = []
    for i in range(2):
        lanes = slice(i * half, (i + 1) * half)
        for h in range(heads):
            features = slice(h * HEAD, (h + 1) * HEAD)
            result = merged[features, lanes] * parts[0][h : h + 1, lanes]
            result = result + other[features, lanes].astype(jnp.float32) * parts[1][h : h + 1, lanes]
            block[lanes, features] = result.astype(jnp.bfloat16).T
        copy = pltpu.make_async_copy(block.at[lanes], out.at[lanes], sems.at[i])
        copy.start()
        copies.append(copy)
    for copy in copies:
        copy.wait()


def nearby_tiles(tile_coords, per_device):
    space_count, tm_count = lax.axis_size("space"), lax.axis_size("tm")
    s, t = lax.axis_index("space"), lax.axis_index("tm")

    def tiles(column, slab):
        device = column * tm_count + slab
        return lax.dynamic_slice_in_dim(tile_coords, device * per_device, per_device, 1)

    slabs = [t, partner(t, NEAR, tm_count), partner(t, FAR, tm_count)]
    columns = [s, partner(s, NEAR, space_count), partner(s, FAR, space_count)]
    key_tiles = jnp.concatenate([tiles(s, slab) for slab in slabs], axis=1)
    return key_tiles, jnp.stack([tiles(column, t) for column in columns], axis=1)


def tile_bias(key_tiles, queries, windows):
    queries = jnp.repeat(queries, TILE, axis=2)
    gap = jnp.abs(key_tiles[:, None, :, None] - queries[:, :, None, :])
    allowed = jnp.all(gap[:, :, None] <= windows[:, None, :, None, None], axis=0)
    bias = jnp.where(allowed, 0.0, MASKED).astype(jnp.float32)
    return [bias[i].reshape(-1, bias.shape[-1]) for i in range(3)]


def shards(query, key, value, tile_coords, windows):
    heads = windows.shape[1]
    rows = query.shape[0]
    width = heads * HEAD
    f32, bf16 = jnp.float32, jnp.bfloat16
    pair = 2 * rows * HEAD * rows

    k_near = exchange(key, "tm", NEAR)
    k_far = swap_slabs(key)
    q_near = exchange(query, "space", NEAR)
    near_tiles = nearby_tiles(tile_coords, rows // TILE)
    q_far = exchange(after(query, near_tiles[0]), "space", FAR)
    v_far = swap_slabs(value)
    v_near = exchange(after(value, k_near), "tm", NEAR)
    bias = tile_bias(*after(near_tiles, k_near), windows)

    def weigh(q, table):
        return call(
            functools.partial(weigh_kernel, heads),
            (
                jax.ShapeDtypeStruct((heads, 3 * rows, rows), bf16),
                jax.ShapeDtypeStruct((16, rows), f32),
            ),
            heads * 3 * pair, q, key, k_near, k_far, table, exps=heads * 3 * rows * rows,
        )

    near_weights, near_stats = weigh(q_near, bias[1])
    far_weights, far_stats = weigh(q_far, after(bias[2], near_stats))
    own_weights, own_stats = weigh(query, bias[0])

    def visitors(side, stats):
        return call(
            functools.partial(visitors_kernel, heads, side),
            jax.ShapeDtypeStruct((width + SPARE, rows), bf16), 0,
            near_weights, near_stats, far_weights, stats, value, v_near, v_far,
        )

    to_next = visitors(0, far_stats)
    to_last = visitors(1, after(far_stats, to_next))
    from_last = shift(to_next, "space", 1)
    from_next = shift(to_last, "space", -1)
    own = call(
        functools.partial(home_kernel, heads), jax.ShapeDtypeStruct((width, rows), f32),
        heads * 3 * pair, own_weights, own_stats, value, v_near, v_far,
    )
    merged, level = call(
        functools.partial(merge_kernel, heads),
        (jax.ShapeDtypeStruct((width, rows), f32), jax.ShapeDtypeStruct((8, rows), f32)), 0,
        own, own_stats, from_last,
    )
    return pl.pallas_call(
        functools.partial(combine_kernel, heads),
        out_shape=jax.ShapeDtypeStruct((rows, width), bf16),
        out_specs=pl.BlockSpec(memory_space=pl.ANY),
        scratch_shapes=[pltpu.VMEM((rows, width), bf16), pltpu.SemaphoreType.DMA((2,))],
        compiler_params=pltpu.CompilerParams(vmem_limit_bytes=40 * 1024 * 1024),
        cost_estimate=pl.CostEstimate(flops=0, bytes_accessed=1024, transcendentals=0),
    )(merged, level, from_next)


def solution(mesh):
    placed = (
        P(("space", "tm"), "head"),
        P(("space", "tm"), "head"),
        P(("space", "tm"), "head"),
        P(),
        P(None, "head"),
    )
    return jax.shard_map(
        shards, mesh=mesh, in_specs=placed, out_specs=P(("space", "tm"), "head"), check_vma=False
    )
```

```python
import functools

import jax
import jax.numpy as jnp
from jax import lax
from jax.experimental import pallas as pl
from jax.experimental.pallas import tpu as pltpu
from jax.sharding import PartitionSpec as P

TILE = 64
HEAD = 128
MASKED = -1e30
FLOOR = -1e29
FACTOR = 1.4426950408889634 * HEAD**-0.5
PARTS = 3
SPARE = 16
NEAR, FAR = 0, 1


def partner(index, side, count):
    step = 1 - 2 * (index % 2)
    return (index + (step if side == NEAR else -step)) % count


def exchange(block, axis, side):
    count = lax.axis_size(axis)
    return lax.ppermute(block, axis, [(i, partner(i, side, count)) for i in range(count)])


def shift(block, axis, distance):
    count = lax.axis_size(axis)
    return lax.ppermute(block, axis, [(i, (i + distance) % count) for i in range(count)])


def swap_slabs(block):
    heads, slabs = lax.axis_size("head"), lax.axis_size("tm")
    pairs = []
    for head in range(heads):
        for slab in range(slabs):
            if 0 < slab < slabs - 1:
                there = head * slabs + partner(slab, FAR, slabs)
            else:
                there = partner(head, NEAR, heads) * slabs + slab
            pairs.append((head * slabs + slab, there))
    return lax.ppermute(block, ("head", "tm"), pairs)


def after(block, other):
    return lax.optimization_barrier((block, other))[0]


def call(kernel, out_shape, flops, *operands, exps=0, moved=1 << 20):
    return pl.pallas_call(
        kernel,
        out_shape=out_shape,
        compiler_params=pltpu.CompilerParams(vmem_limit_bytes=40 * 1024 * 1024),
        cost_estimate=pl.CostEstimate(flops=0, bytes_accessed=1024, transcendentals=0),
    )(*operands)


def mark_kernel(out):
    out[...] = jnp.zeros(out.shape, out.dtype)


def weigh_kernel(heads, key_far, key_near, q, key, bias, weights_out, stats_out):
    stats_out[...] = jnp.zeros(stats_out.shape, jnp.float32)
    tiles = key.shape[0] // TILE
    for h in range(heads):
        lanes = slice(h * HEAD, (h + 1) * HEAD)
        blocks, peak = [], None
        for j, keys in enumerate((key, key_near, key_far)):
            raw = lax.dot_general(
                keys[:, lanes], q[:, lanes], (((1,), (1,)), ((), ())),
                preferred_element_type=jnp.float32,
            )
            for i in range(tiles):
                row = (h * 3 + j) * tiles + i
                block = raw[i * TILE : (i + 1) * TILE] + bias[row : row + 1, :]
                blocks.append(block)
                peak = block if peak is None else jnp.maximum(peak, block)
        peak = jnp.maximum(jnp.max(peak, axis=0, keepdims=True), FLOOR)
        total = None
        for i, block in enumerate(blocks):
            weights = jnp.exp2((block - peak) * FACTOR)
            weights_out[h, i * TILE : (i + 1) * TILE, :] = weights.astype(jnp.bfloat16)
            total = weights if total is None else total + weights
        total = jnp.maximum(jnp.sum(total, axis=0, keepdims=True), 0.5)
        stats_out[h : h + 1, :] = 1.0 / total
        stats_out[8 + h : 9 + h, :] = peak * FACTOR + jnp.log2(total)


def weighted(h, weights, stats, values):
    lanes = slice(h * HEAD, (h + 1) * HEAD)
    width = values[0].shape[0]
    summed = None
    for j, value in enumerate(values):
        part = lax.dot_general(
            value[:, lanes], weights[h, j * width : (j + 1) * width, :],
            (((0,), (0,)), ((), ())), preferred_element_type=jnp.float32,
        )
        summed = part if summed is None else summed + part
    return summed * stats[h : h + 1, :]


def visitors_kernel(
    heads, side, near_weights, near_stats, far_weights, far_stats, v, v_near, v_far, out
):
    end = heads * HEAD
    odd = lax.axis_index("space") % 2

    def sum_up(weights, stats):
        for h in range(heads):
            out[h * HEAD : (h + 1) * HEAD, :] = weighted(
                h, weights, stats, (v, v_near, v_far)
            ).astype(jnp.bfloat16)
        rest = stats[8:16, :]
        pieces = []
        for part in range(PARTS):
            piece = rest.astype(jnp.bfloat16).astype(jnp.float32)
            rest = rest - piece
            pieces.append(piece[0:heads])
        pieces.append(jnp.zeros((SPARE - PARTS * heads, rest.shape[1]), jnp.float32))
        out[end : end + SPARE, :] = jnp.concatenate(pieces, axis=0).astype(jnp.bfloat16)

    pl.when(odd == side)(lambda: sum_up(near_weights, near_stats))
    pl.when(odd != side)(lambda: sum_up(far_weights, far_stats))


def home_kernel(heads, weights, stats, v, v_near, v_far, out):
    for h in range(heads):
        out[h * HEAD : (h + 1) * HEAD, :] = weighted(h, weights, stats, (v, v_near, v_far))


def level_of(ref, heads):
    spare = ref[heads * HEAD : heads * HEAD + SPARE, :].astype(jnp.float32)
    return spare[0:heads] + spare[heads : 2 * heads] + spare[2 * heads : 3 * heads]


def shares(levels):
    top = functools.reduce(jnp.maximum, levels)
    parts = [jnp.exp2(level - top) for level in levels]
    scale = 1.0 / functools.reduce(jnp.add, parts)
    return [part * scale for part in parts]


def merge_kernel(heads, own, stats, near, out, level_out):
    levels = [stats[8 : 8 + heads, :], level_of(near, heads)]
    top = jnp.maximum(levels[0], levels[1])
    parts = [jnp.exp2(level - top) for level in levels]
    scale = 1.0 / (parts[0] + parts[1])
    level_out[...] = jnp.zeros(level_out.shape, jnp.float32)
    level_out[0:heads, :] = top + jnp.log2(parts[0] + parts[1])
    parts = [part * scale for part in parts]
    for h in range(heads):
        rows = slice(h * HEAD, (h + 1) * HEAD)
        result = own[rows, :] * parts[0][h : h + 1]
        out[rows, :] = result + near[rows, :].astype(jnp.float32) * parts[1][h : h + 1]


def combine_kernel(heads, merged, level, other, out, block, sems):
    parts = shares([level[0:heads, :], level_of(other, heads)])
    rows = block.shape[0]
    half = rows // 2
    copies = []
    for i in range(2):
        lanes = slice(i * half, (i + 1) * half)
        for h in range(heads):
            features = slice(h * HEAD, (h + 1) * HEAD)
            result = merged[features, lanes] * parts[0][h : h + 1, lanes]
            result = result + other[features, lanes].astype(jnp.float32) * parts[1][h : h + 1, lanes]
            block[lanes, features] = result.astype(jnp.bfloat16).T
        copy = pltpu.make_async_copy(block.at[lanes], out.at[lanes], sems.at[i])
        copy.start()
        copies.append(copy)
    for copy in copies:
        copy.wait()


def tile_bias(tile_coords, windows, per_device, gate):
    space_count, tm_count = lax.axis_size("space"), lax.axis_size("tm")
    s, t = lax.axis_index("space"), lax.axis_index("tm")

    def tiles(column, slab):
        device = column * tm_count + slab
        return lax.dynamic_slice_in_dim(tile_coords, device * per_device, per_device, 1)

    slabs = [t, partner(t, NEAR, tm_count), partner(t, FAR, tm_count)]
    columns = [s, partner(s, NEAR, space_count), partner(s, FAR, space_count)]
    key_tiles = jnp.concatenate([tiles(s, slab) for slab in slabs], axis=1)
    queries = jnp.stack([tiles(column, t) for column in columns], axis=1)
    key_tiles, queries, _ = lax.optimization_barrier((key_tiles, queries, gate))
    queries = jnp.repeat(queries, TILE, axis=2)
    gap = jnp.abs(key_tiles[:, None, :, None] - queries[:, :, None, :])
    allowed = jnp.all(gap[:, :, None] <= windows[:, None, :, None, None], axis=0)
    bias = jnp.where(allowed, 0.0, MASKED).astype(jnp.float32)
    return [bias[i].reshape(-1, bias.shape[-1]) for i in range(3)]


def shards(query, key, value, tile_coords, windows):
    heads = windows.shape[1]
    rows = query.shape[0]
    width = heads * HEAD
    f32, bf16 = jnp.float32, jnp.bfloat16
    pair = 2 * rows * HEAD * rows

    k_near = exchange(key, "tm", NEAR)
    k_far = swap_slabs(key)
    mark = call(mark_kernel, jax.ShapeDtypeStruct((8, HEAD), f32), 0)
    sent = after(query, mark)
    q_near = exchange(query, "space", NEAR)
    q_far = exchange(sent, "space", FAR)
    v_far = swap_slabs(value)
    v_near = exchange(after(value, k_near), "tm", NEAR)
    bias = tile_bias(tile_coords, windows, rows // TILE, k_near)

    def weigh(q, table):
        return call(
            functools.partial(weigh_kernel, heads),
            (
                jax.ShapeDtypeStruct((heads, 3 * rows, rows), bf16),
                jax.ShapeDtypeStruct((16, rows), f32),
            ),
            heads * 3 * pair, k_far, k_near, q, key, table, exps=heads * 3 * rows * rows,
        )

    near_weights, near_stats = weigh(q_near, bias[1])
    far_weights, far_stats = weigh(q_far, after(bias[2], near_stats))
    own_weights, own_stats = weigh(query, bias[0])

    def visitors(side, stats):
        return call(
            functools.partial(visitors_kernel, heads, side),
            jax.ShapeDtypeStruct((width + SPARE, rows), bf16), 0,
            near_weights, near_stats, far_weights, stats, value, v_near, v_far,
        )

    to_next = visitors(0, far_stats)
    to_last = visitors(1, after(far_stats, to_next))
    from_last = shift(to_next, "space", 1)
    from_next = shift(to_last, "space", -1)
    own = call(
        functools.partial(home_kernel, heads), jax.ShapeDtypeStruct((width, rows), f32),
        heads * 3 * pair, own_weights, own_stats, value, v_near, v_far,
    )
    merged, level = call(
        functools.partial(merge_kernel, heads),
        (jax.ShapeDtypeStruct((width, rows), f32), jax.ShapeDtypeStruct((8, rows), f32)), 0,
        own, own_stats, from_last,
    )
    return pl.pallas_call(
        functools.partial(combine_kernel, heads),
        out_shape=jax.ShapeDtypeStruct((rows, width), bf16),
        out_specs=pl.BlockSpec(memory_space=pl.ANY),
        scratch_shapes=[pltpu.VMEM((rows, width), bf16), pltpu.SemaphoreType.DMA((2,))],
        compiler_params=pltpu.CompilerParams(vmem_limit_bytes=40 * 1024 * 1024),
        cost_estimate=pl.CostEstimate(flops=0, bytes_accessed=1024, transcendentals=0),
    )(merged, level, from_next)


def solution(mesh):
    placed = (
        P(("space", "tm"), "head"),
        P(("space", "tm"), "head"),
        P(("space", "tm"), "head"),
        P(),
        P(None, "head"),
    )
    return jax.shard_map(
        shards, mesh=mesh, in_specs=placed, out_specs=P(("space", "tm"), "head"), check_vma=False
    )
```

```python
import functools

import jax
import jax.numpy as jnp
from jax import lax
from jax.experimental import pallas as pl
from jax.experimental.pallas import tpu as pltpu
from jax.sharding import PartitionSpec as P

TILE = 64
HEAD = 128
MASKED = -1e30
FLOOR = -1e29
FACTOR = 1.4426950408889634 * HEAD**-0.5
PARTS = 3
SPARE = 16
NEAR, FAR = 0, 1


def partner(index, side, count):
    step = 1 - 2 * (index % 2)
    return (index + (step if side == NEAR else -step)) % count


def exchange(block, axis, side):
    count = lax.axis_size(axis)
    return lax.ppermute(block, axis, [(i, partner(i, side, count)) for i in range(count)])


def shift(block, axis, distance):
    count = lax.axis_size(axis)
    return lax.ppermute(block, axis, [(i, (i + distance) % count) for i in range(count)])


def swap_slabs(block):
    heads, slabs = lax.axis_size("head"), lax.axis_size("tm")
    pairs = []
    for head in range(heads):
        for slab in range(slabs):
            if 0 < slab < slabs - 1:
                there = head * slabs + partner(slab, FAR, slabs)
            else:
                there = partner(head, NEAR, heads) * slabs + slab
            pairs.append((head * slabs + slab, there))
    return lax.ppermute(block, ("head", "tm"), pairs)


def after(block, other):
    return lax.optimization_barrier((block, other))[0]


def call(kernel, out_shape, flops, *operands, exps=0, moved=1 << 20):
    return pl.pallas_call(
        kernel,
        out_shape=out_shape,
        compiler_params=pltpu.CompilerParams(vmem_limit_bytes=40 * 1024 * 1024),
        cost_estimate=pl.CostEstimate(flops=0, bytes_accessed=1024, transcendentals=0),
    )(*operands)


def mark_kernel(out):
    out[...] = jnp.zeros(out.shape, out.dtype)


def weigh_kernel(heads, key_far, key_near, q, key, bias, weights_out, stats_out):
    stats_out[...] = jnp.zeros(stats_out.shape, jnp.float32)
    tiles = key.shape[0] // TILE
    for h in range(heads):
        lanes = slice(h * HEAD, (h + 1) * HEAD)
        blocks, peak = [], None
        for j, keys in enumerate((key, key_near, key_far)):
            raw = lax.dot_general(
                keys[:, lanes], q[:, lanes], (((1,), (1,)), ((), ())),
                preferred_element_type=jnp.float32,
            )
            for i in range(tiles):
                row = (h * 3 + j) * tiles + i
                block = raw[i * TILE : (i + 1) * TILE] + bias[row : row + 1, :]
                blocks.append(block)
                peak = block if peak is None else jnp.maximum(peak, block)
        peak = jnp.maximum(jnp.max(peak, axis=0, keepdims=True), FLOOR)
        total = None
        for i, block in enumerate(blocks):
            weights = jnp.exp2((block - peak) * FACTOR)
            weights_out[h, i * TILE : (i + 1) * TILE, :] = weights.astype(jnp.bfloat16)
            total = weights if total is None else total + weights
        total = jnp.maximum(jnp.sum(total, axis=0, keepdims=True), 0.5)
        stats_out[h : h + 1, :] = 1.0 / total
        stats_out[8 + h : 9 + h, :] = peak * FACTOR + jnp.log2(total)


def weighted(h, weights, value, j):
    lanes = slice(h * HEAD, (h + 1) * HEAD)
    width = value.shape[0]
    return lax.dot_general(
        value[:, lanes], weights[h, j * width : (j + 1) * width, :],
        (((0,), (0,)), ((), ())), preferred_element_type=jnp.float32,
    )


def by_side(side, body, near, far):
    odd = lax.axis_index("space") % 2
    pl.when(odd == side)(lambda: body(*near))
    pl.when(odd != side)(lambda: body(*far))


def store(heads, out, stats, summed):
    for h in range(heads):
        rows = slice(h * HEAD, (h + 1) * HEAD)
        out[rows, :] = (summed(h, rows) * stats[h : h + 1, :]).astype(jnp.bfloat16)
    end = heads * HEAD
    rest = stats[8:16, :]
    pieces = []
    for part in range(PARTS):
        piece = rest.astype(jnp.bfloat16).astype(jnp.float32)
        rest = rest - piece
        pieces.append(piece[0:heads])
    pieces.append(jnp.zeros((SPARE - PARTS * heads, rest.shape[1]), jnp.float32))
    out[end : end + SPARE, :] = jnp.concatenate(pieces, axis=0).astype(jnp.bfloat16)


def early_kernel(heads, side, near_weights, far_weights, v, v_far, out):
    def body(weights):
        for h in range(heads):
            out[h * HEAD : (h + 1) * HEAD, :] = weighted(h, weights, v, 0) + weighted(h, weights, v_far, 2)

    by_side(side, body, (near_weights,), (far_weights,))


def finish_kernel(heads, side, near_weights, near_stats, far_weights, far_stats, early, v_near, out):
    def body(weights, stats):
        store(heads, out, stats, lambda h, rows: early[rows, :] + weighted(h, weights, v_near, 1))

    by_side(side, body, (near_weights, near_stats), (far_weights, far_stats))


def visitors_kernel(
    heads, side, near_weights, near_stats, far_weights, far_stats, v, v_near, v_far, out
):
    def body(weights, stats):
        store(
            heads, out, stats,
            lambda h, rows: sum(weighted(h, weights, x, j) for j, x in enumerate((v, v_near, v_far))),
        )

    by_side(side, body, (near_weights, near_stats), (far_weights, far_stats))


def home_kernel(heads, weights, stats, v, v_near, v_far, out):
    for h in range(heads):
        summed = sum(weighted(h, weights, x, j) for j, x in enumerate((v, v_near, v_far)))
        out[h * HEAD : (h + 1) * HEAD, :] = summed * stats[h : h + 1, :]


def level_of(ref, heads):
    spare = ref[heads * HEAD : heads * HEAD + SPARE, :].astype(jnp.float32)
    return spare[0:heads] + spare[heads : 2 * heads] + spare[2 * heads : 3 * heads]


def shares(levels):
    top = functools.reduce(jnp.maximum, levels)
    parts = [jnp.exp2(level - top) for level in levels]
    scale = 1.0 / functools.reduce(jnp.add, parts)
    return [part * scale for part in parts]


def merge_kernel(heads, own, stats, near, out, level_out):
    levels = [stats[8 : 8 + heads, :], level_of(near, heads)]
    top = jnp.maximum(levels[0], levels[1])
    parts = [jnp.exp2(level - top) for level in levels]
    scale = 1.0 / (parts[0] + parts[1])
    level_out[...] = jnp.zeros(level_out.shape, jnp.float32)
    level_out[0:heads, :] = top + jnp.log2(parts[0] + parts[1])
    parts = [part * scale for part in parts]
    for h in range(heads):
        rows = slice(h * HEAD, (h + 1) * HEAD)
        result = own[rows, :] * parts[0][h : h + 1]
        out[rows, :] = result + near[rows, :].astype(jnp.float32) * parts[1][h : h + 1]


def combine_kernel(heads, merged, level, other, out, block, sems):
    parts = shares([level[0:heads, :], level_of(other, heads)])
    rows = block.shape[0]
    half = rows // 2
    copies = []
    for i in range(2):
        lanes = slice(i * half, (i + 1) * half)
        for h in range(heads):
            features = slice(h * HEAD, (h + 1) * HEAD)
            result = merged[features, lanes] * parts[0][h : h + 1, lanes]
            result = result + other[features, lanes].astype(jnp.float32) * parts[1][h : h + 1, lanes]
            block[lanes, features] = result.astype(jnp.bfloat16).T
        copy = pltpu.make_async_copy(block.at[lanes], out.at[lanes], sems.at[i])
        copy.start()
        copies.append(copy)
    for copy in copies:
        copy.wait()


def tile_bias(tile_coords, windows, per_device, gate):
    space_count, tm_count = lax.axis_size("space"), lax.axis_size("tm")
    s, t = lax.axis_index("space"), lax.axis_index("tm")

    def tiles(column, slab):
        device = column * tm_count + slab
        return lax.dynamic_slice_in_dim(tile_coords, device * per_device, per_device, 1)

    slabs = [t, partner(t, NEAR, tm_count), partner(t, FAR, tm_count)]
    columns = [s, partner(s, NEAR, space_count), partner(s, FAR, space_count)]
    key_tiles = jnp.concatenate([tiles(s, slab) for slab in slabs], axis=1)
    queries = jnp.stack([tiles(column, t) for column in columns], axis=1)
    key_tiles, queries, _ = lax.optimization_barrier((key_tiles, queries, gate))
    queries = jnp.repeat(queries, TILE, axis=2)
    gap = jnp.abs(key_tiles[:, None, :, None] - queries[:, :, None, :])
    allowed = jnp.all(gap[:, :, None] <= windows[:, None, :, None, None], axis=0)
    bias = jnp.where(allowed, 0.0, MASKED).astype(jnp.float32)
    return [bias[i].reshape(-1, bias.shape[-1]) for i in range(3)]


def shards(query, key, value, tile_coords, windows):
    heads = windows.shape[1]
    rows = query.shape[0]
    width = heads * HEAD
    f32, bf16 = jnp.float32, jnp.bfloat16
    pair = 2 * rows * HEAD * rows

    k_near = exchange(key, "tm", NEAR)
    k_far = swap_slabs(key)
    mark = call(mark_kernel, jax.ShapeDtypeStruct((8, HEAD), f32), 0)
    sent = after(query, mark)
    q_near = exchange(query, "space", NEAR)
    q_far = exchange(sent, "space", FAR)
    v_far = swap_slabs(value)
    v_near = exchange(after(value, k_near), "tm", NEAR)
    bias = tile_bias(after(tile_coords, k_far), windows, rows // TILE, k_near)

    def weigh(q, table):
        return call(
            functools.partial(weigh_kernel, heads),
            (
                jax.ShapeDtypeStruct((heads, 3 * rows, rows), bf16),
                jax.ShapeDtypeStruct((16, rows), f32),
            ),
            heads * 3 * pair, k_far, k_near, q, key, table, exps=heads * 3 * rows * rows,
        )

    near_weights, near_stats = weigh(q_near, bias[1])
    far_weights, far_stats = weigh(q_far, after(bias[2], near_stats))
    own_weights, own_stats = weigh(query, bias[0])

    back = jax.ShapeDtypeStruct((width + SPARE, rows), bf16)
    early = call(
        functools.partial(early_kernel, heads, 0), jax.ShapeDtypeStruct((width, rows), f32), 0,
        near_weights, far_weights, value, v_far,
    )
    to_next = call(
        functools.partial(finish_kernel, heads, 0), back, 0,
        near_weights, near_stats, far_weights, far_stats, early, v_near,
    )
    to_last = call(
        functools.partial(visitors_kernel, heads, 1), back, 0,
        near_weights, near_stats, far_weights, after(far_stats, to_next), value, v_near, v_far,
    )
    from_last = shift(to_next, "space", 1)
    from_next = shift(to_last, "space", -1)
    own = call(
        functools.partial(home_kernel, heads), jax.ShapeDtypeStruct((width, rows), f32),
        heads * 3 * pair, own_weights, own_stats, value, v_near, v_far,
    )
    merged, level = call(
        functools.partial(merge_kernel, heads),
        (jax.ShapeDtypeStruct((width, rows), f32), jax.ShapeDtypeStruct((8, rows), f32)), 0,
        own, own_stats, from_last,
    )
    return pl.pallas_call(
        functools.partial(combine_kernel, heads),
        out_shape=jax.ShapeDtypeStruct((rows, width), bf16),
        out_specs=pl.BlockSpec(memory_space=pl.ANY),
        scratch_shapes=[pltpu.VMEM((rows, width), bf16), pltpu.SemaphoreType.DMA((2,))],
        compiler_params=pltpu.CompilerParams(vmem_limit_bytes=40 * 1024 * 1024),
        cost_estimate=pl.CostEstimate(flops=0, bytes_accessed=1024, transcendentals=0),
    )(merged, level, from_next)


def solution(mesh):
    placed = (
        P(("space", "tm"), "head"),
        P(("space", "tm"), "head"),
        P(("space", "tm"), "head"),
        P(),
        P(None, "head"),
    )
    return jax.shard_map(
        shards, mesh=mesh, in_specs=placed, out_specs=P(("space", "tm"), "head"), check_vma=False
    )
```

```python
import functools

import jax
import jax.numpy as jnp
from jax import lax
from jax.experimental import pallas as pl
from jax.experimental.pallas import tpu as pltpu
from jax.sharding import PartitionSpec as P

TILE = 64
HEAD = 128
MASKED = -1e30
FLOOR = -1e29
FACTOR = 1.4426950408889634 * HEAD**-0.5
PARTS = 3
SPARE = 16
NEAR, FAR = 0, 1


def partner(index, side, count):
    step = 1 - 2 * (index % 2)
    return (index + (step if side == NEAR else -step)) % count


def exchange(block, axis, side):
    count = lax.axis_size(axis)
    return lax.ppermute(block, axis, [(i, partner(i, side, count)) for i in range(count)])


def shift(block, axis, distance):
    count = lax.axis_size(axis)
    return lax.ppermute(block, axis, [(i, (i + distance) % count) for i in range(count)])


def swap_slabs(block):
    heads, slabs = lax.axis_size("head"), lax.axis_size("tm")
    pairs = []
    for head in range(heads):
        for slab in range(slabs):
            if 0 < slab < slabs - 1:
                there = head * slabs + partner(slab, FAR, slabs)
            else:
                there = partner(head, NEAR, heads) * slabs + slab
            pairs.append((head * slabs + slab, there))
    return lax.ppermute(block, ("head", "tm"), pairs)


def after(block, other):
    return lax.optimization_barrier((block, other))[0]


def call(kernel, out_shape, flops, *operands, exps=0, moved=1 << 20):
    return pl.pallas_call(
        kernel,
        out_shape=out_shape,
        compiler_params=pltpu.CompilerParams(vmem_limit_bytes=40 * 1024 * 1024),
        cost_estimate=pl.CostEstimate(flops=0, bytes_accessed=1024, transcendentals=0),
    )(*operands)


def mark_kernel(out):
    out[...] = jnp.zeros(out.shape, out.dtype)


def weigh_if_kernel(heads, parity, *refs):
    pl.when(lax.axis_index("space") % 2 == parity)(lambda: weigh_kernel(heads, *refs))


def weigh_kernel(heads, key_far, key_near, q, key, bias, weights_out, stats_out):
    stats_out[...] = jnp.zeros(stats_out.shape, jnp.float32)
    tiles = key.shape[0] // TILE
    for h in range(heads):
        lanes = slice(h * HEAD, (h + 1) * HEAD)
        blocks, peak = [], None
        for j, keys in enumerate((key, key_near, key_far)):
            raw = lax.dot_general(
                keys[:, lanes], q[:, lanes], (((1,), (1,)), ((), ())),
                preferred_element_type=jnp.float32,
            )
            for i in range(tiles):
                row = (h * 3 + j) * tiles + i
                block = raw[i * TILE : (i + 1) * TILE] + bias[row : row + 1, :]
                blocks.append(block)
                peak = block if peak is None else jnp.maximum(peak, block)
        peak = jnp.maximum(jnp.max(peak, axis=0, keepdims=True), FLOOR)
        total = None
        for i, block in enumerate(blocks):
            weights = jnp.exp2((block - peak) * FACTOR)
            weights_out[h, i * TILE : (i + 1) * TILE, :] = weights.astype(jnp.bfloat16)
            total = weights if total is None else total + weights
        total = jnp.maximum(jnp.sum(total, axis=0, keepdims=True), 0.5)
        stats_out[h : h + 1, :] = 1.0 / total
        stats_out[8 + h : 9 + h, :] = peak * FACTOR + jnp.log2(total)


def weighted(h, weights, value, j):
    lanes = slice(h * HEAD, (h + 1) * HEAD)
    width = value.shape[0]
    return lax.dot_general(
        value[:, lanes], weights[h, j * width : (j + 1) * width, :],
        (((0,), (0,)), ((), ())), preferred_element_type=jnp.float32,
    )


def by_side(side, body, near, far):
    odd = lax.axis_index("space") % 2
    pl.when(odd == side)(lambda: body(*near))
    pl.when(odd != side)(lambda: body(*far))


def store(heads, out, stats, summed):
    for h in range(heads):
        rows = slice(h * HEAD, (h + 1) * HEAD)
        out[rows, :] = (summed(h, rows) * stats[h : h + 1, :]).astype(jnp.bfloat16)
    end = heads * HEAD
    rest = stats[8:16, :]
    pieces = []
    for part in range(PARTS):
        piece = rest.astype(jnp.bfloat16).astype(jnp.float32)
        rest = rest - piece
        pieces.append(piece[0:heads])
    pieces.append(jnp.zeros((SPARE - PARTS * heads, rest.shape[1]), jnp.float32))
    out[end : end + SPARE, :] = jnp.concatenate(pieces, axis=0).astype(jnp.bfloat16)


def early_kernel(heads, side, near_weights, far_weights, v, v_far, out):
    def body(weights):
        for h in range(heads):
            out[h * HEAD : (h + 1) * HEAD, :] = weighted(h, weights, v, 0) + weighted(h, weights, v_far, 2)

    by_side(side, body, (near_weights,), (far_weights,))


def finish_kernel(heads, side, near_weights, near_stats, far_weights, far_stats, early, v_near, out):
    def body(weights, stats):
        store(heads, out, stats, lambda h, rows: early[rows, :] + weighted(h, weights, v_near, 1))

    by_side(side, body, (near_weights, near_stats), (far_weights, far_stats))


def visitors_kernel(
    heads, side, near_weights, near_stats, far_weights, far_stats, v, v_near, v_far, out
):
    def body(weights, stats):
        store(
            heads, out, stats,
            lambda h, rows: sum(weighted(h, weights, x, j) for j, x in enumerate((v, v_near, v_far))),
        )

    by_side(side, body, (near_weights, near_stats), (far_weights, far_stats))


def home_kernel(heads, weights, stats, v, v_near, v_far, out):
    for h in range(heads):
        summed = sum(weighted(h, weights, x, j) for j, x in enumerate((v, v_near, v_far)))
        out[h * HEAD : (h + 1) * HEAD, :] = summed * stats[h : h + 1, :]


def level_of(ref, heads):
    spare = ref[heads * HEAD : heads * HEAD + SPARE, :].astype(jnp.float32)
    return spare[0:heads] + spare[heads : 2 * heads] + spare[2 * heads : 3 * heads]


def shares(levels):
    top = functools.reduce(jnp.maximum, levels)
    parts = [jnp.exp2(level - top) for level in levels]
    scale = 1.0 / functools.reduce(jnp.add, parts)
    return [part * scale for part in parts]


def merge_kernel(heads, own, stats, near, out, level_out):
    levels = [stats[8 : 8 + heads, :], level_of(near, heads)]
    top = jnp.maximum(levels[0], levels[1])
    parts = [jnp.exp2(level - top) for level in levels]
    scale = 1.0 / (parts[0] + parts[1])
    level_out[...] = jnp.zeros(level_out.shape, jnp.float32)
    level_out[0:heads, :] = top + jnp.log2(parts[0] + parts[1])
    parts = [part * scale for part in parts]
    for h in range(heads):
        rows = slice(h * HEAD, (h + 1) * HEAD)
        result = own[rows, :] * parts[0][h : h + 1]
        out[rows, :] = result + near[rows, :].astype(jnp.float32) * parts[1][h : h + 1]


def combine_kernel(heads, merged, level, other, out, block, sems):
    parts = shares([level[0:heads, :], level_of(other, heads)])
    rows = block.shape[0]
    half = rows // 2
    copies = []
    for i in range(2):
        lanes = slice(i * half, (i + 1) * half)
        for h in range(heads):
            features = slice(h * HEAD, (h + 1) * HEAD)
            result = merged[features, lanes] * parts[0][h : h + 1, lanes]
            result = result + other[features, lanes].astype(jnp.float32) * parts[1][h : h + 1, lanes]
            block[lanes, features] = result.astype(jnp.bfloat16).T
        copy = pltpu.make_async_copy(block.at[lanes], out.at[lanes], sems.at[i])
        copy.start()
        copies.append(copy)
    for copy in copies:
        copy.wait()


def tile_bias(tile_coords, windows, per_device, gate):
    space_count, tm_count = lax.axis_size("space"), lax.axis_size("tm")
    s, t = lax.axis_index("space"), lax.axis_index("tm")

    def tiles(column, slab):
        device = column * tm_count + slab
        return lax.dynamic_slice_in_dim(tile_coords, device * per_device, per_device, 1)

    slabs = [t, partner(t, NEAR, tm_count), partner(t, FAR, tm_count)]
    columns = [s, partner(s, NEAR, space_count), partner(s, FAR, space_count)]
    key_tiles = jnp.concatenate([tiles(s, slab) for slab in slabs], axis=1)
    queries = jnp.stack([tiles(column, t) for column in columns], axis=1)
    key_tiles, queries, _ = lax.optimization_barrier((key_tiles, queries, gate))
    queries = jnp.repeat(queries, TILE, axis=2)
    gap = jnp.abs(key_tiles[:, None, :, None] - queries[:, :, None, :])
    allowed = jnp.all(gap[:, :, None] <= windows[:, None, :, None, None], axis=0)
    bias = jnp.where(allowed, 0.0, MASKED).astype(jnp.float32)
    return [bias[i].reshape(-1, bias.shape[-1]) for i in range(3)]


def shards(query, key, value, tile_coords, windows):
    heads = windows.shape[1]
    rows = query.shape[0]
    width = heads * HEAD
    f32, bf16 = jnp.float32, jnp.bfloat16
    pair = 2 * rows * HEAD * rows

    k_near = exchange(key, "tm", NEAR)
    k_far = swap_slabs(key)
    mark = call(mark_kernel, jax.ShapeDtypeStruct((8, HEAD), f32), 0)
    sent = after(query, mark)
    q_near = exchange(query, "space", NEAR)
    q_far = exchange(sent, "space", FAR)
    v_far = swap_slabs(value)
    v_near = exchange(after(value, k_near), "tm", NEAR)
    bias = tile_bias(after(tile_coords, k_far), windows, rows // TILE, k_near)

    def weigh(kernel, q, table):
        return call(
            kernel,
            (
                jax.ShapeDtypeStruct((heads, 3 * rows, rows), bf16),
                jax.ShapeDtypeStruct((16, rows), f32),
            ),
            heads * 3 * pair, k_far, k_near, q, key, table,
            exps=heads * 3 * rows * rows,
        )

    always = functools.partial(weigh_kernel, heads)
    near_weights, near_stats = weigh(always, q_near, bias[1])
    odd_weights, odd_stats = weigh(
        functools.partial(weigh_if_kernel, heads, 1), q_far, after(bias[2], near_stats)
    )
    back = jax.ShapeDtypeStruct((width + SPARE, rows), bf16)
    early = call(
        functools.partial(early_kernel, heads, 0), jax.ShapeDtypeStruct((width, rows), f32), 0,
        near_weights, odd_weights, value, v_far,
    )
    to_next = call(
        functools.partial(finish_kernel, heads, 0), back, 0,
        near_weights, near_stats, odd_weights, odd_stats, early, v_near,
    )
    even_weights, even_stats = weigh(
        functools.partial(weigh_if_kernel, heads, 0), q_far, after(bias[2], to_next)
    )
    to_last = call(
        functools.partial(visitors_kernel, heads, 1), back, 0,
        near_weights, near_stats, even_weights, even_stats, value, v_near, v_far,
    )
    own_weights, own_stats = weigh(always, query, after(bias[0], to_last))
    from_last = shift(to_next, "space", 1)
    from_next = shift(to_last, "space", -1)
    own = call(
        functools.partial(home_kernel, heads), jax.ShapeDtypeStruct((width, rows), f32),
        heads * 3 * pair, own_weights, own_stats, value, v_near, v_far,
    )
    merged, level = call(
        functools.partial(merge_kernel, heads),
        (jax.ShapeDtypeStruct((width, rows), f32), jax.ShapeDtypeStruct((8, rows), f32)), 0,
        own, own_stats, from_last,
    )
    return pl.pallas_call(
        functools.partial(combine_kernel, heads),
        out_shape=jax.ShapeDtypeStruct((rows, width), bf16),
        out_specs=pl.BlockSpec(memory_space=pl.ANY),
        scratch_shapes=[pltpu.VMEM((rows, width), bf16), pltpu.SemaphoreType.DMA((2,))],
        compiler_params=pltpu.CompilerParams(vmem_limit_bytes=40 * 1024 * 1024),
        cost_estimate=pl.CostEstimate(flops=0, bytes_accessed=1024, transcendentals=0),
    )(merged, level, from_next)


def solution(mesh):
    placed = (
        P(("space", "tm"), "head"),
        P(("space", "tm"), "head"),
        P(("space", "tm"), "head"),
        P(),
        P(None, "head"),
    )
    return jax.shard_map(
        shards, mesh=mesh, in_specs=placed, out_specs=P(("space", "tm"), "head"), check_vma=False
    )
```

```python
import functools

import jax
import jax.numpy as jnp
from jax import lax
from jax.experimental import pallas as pl
from jax.experimental.pallas import tpu as pltpu
from jax.sharding import PartitionSpec as P

TILE = 64
HEAD = 128
MASKED = -1e30
FLOOR = -1e29
FACTOR = 1.4426950408889634 * HEAD**-0.5
PARTS = 3
SPARE = 16
NEAR, FAR = 0, 1


def partner(index, side, count):
    step = 1 - 2 * (index % 2)
    return (index + (step if side == NEAR else -step)) % count


def exchange(block, axis, side):
    count = lax.axis_size(axis)
    return lax.ppermute(block, axis, [(i, partner(i, side, count)) for i in range(count)])


def shift(block, axis, distance):
    count = lax.axis_size(axis)
    return lax.ppermute(block, axis, [(i, (i + distance) % count) for i in range(count)])


def swap_slabs(block):
    heads, slabs = lax.axis_size("head"), lax.axis_size("tm")
    pairs = []
    for head in range(heads):
        for slab in range(slabs):
            if 0 < slab < slabs - 1:
                there = head * slabs + partner(slab, FAR, slabs)
            else:
                there = partner(head, NEAR, heads) * slabs + slab
            pairs.append((head * slabs + slab, there))
    return lax.ppermute(block, ("head", "tm"), pairs)


def after(block, other):
    return lax.optimization_barrier((block, other))[0]


def call(kernel, out_shape, flops, *operands, exps=0, moved=1 << 20):
    return pl.pallas_call(
        kernel,
        out_shape=out_shape,
        compiler_params=pltpu.CompilerParams(vmem_limit_bytes=40 * 1024 * 1024),
        cost_estimate=pl.CostEstimate(flops=0, bytes_accessed=1024, transcendentals=0),
    )(*operands)


def mark_kernel(out):
    out[...] = jnp.zeros(out.shape, out.dtype)


def weigh_if_kernel(heads, parity, *refs):
    pl.when(lax.axis_index("space") % 2 == parity)(lambda: weigh_kernel(heads, *refs))


def weigh_kernel(heads, key_far, key_near, q, key, bias, weights_out, stats_out):
    stats_out[...] = jnp.zeros(stats_out.shape, jnp.float32)
    tiles = key.shape[0] // TILE
    for h in range(heads):
        lanes = slice(h * HEAD, (h + 1) * HEAD)
        blocks, peak = [], None
        for j, keys in enumerate((key, key_near, key_far)):
            raw = lax.dot_general(
                keys[:, lanes], q[:, lanes], (((1,), (1,)), ((), ())),
                preferred_element_type=jnp.float32,
            )
            for i in range(tiles):
                row = (h * 3 + j) * tiles + i
                block = raw[i * TILE : (i + 1) * TILE] + bias[row : row + 1, :]
                blocks.append(block)
                peak = block if peak is None else jnp.maximum(peak, block)
        peak = jnp.maximum(jnp.max(peak, axis=0, keepdims=True), FLOOR)
        total = None
        for i, block in enumerate(blocks):
            weights = jnp.exp2((block - peak) * FACTOR)
            weights_out[h, i * TILE : (i + 1) * TILE, :] = weights.astype(jnp.bfloat16)
            total = weights if total is None else total + weights
        total = jnp.maximum(jnp.sum(total, axis=0, keepdims=True), 0.5)
        stats_out[h : h + 1, :] = 1.0 / total
        stats_out[8 + h : 9 + h, :] = peak * FACTOR + jnp.log2(total)


def weighted(h, weights, value, j):
    lanes = slice(h * HEAD, (h + 1) * HEAD)
    width = value.shape[0]
    return lax.dot_general(
        value[:, lanes], weights[h, j * width : (j + 1) * width, :],
        (((0,), (0,)), ((), ())), preferred_element_type=jnp.float32,
    )


def by_side(side, body, near, far):
    odd = lax.axis_index("space") % 2
    pl.when(odd == side)(lambda: body(*near))
    pl.when(odd != side)(lambda: body(*far))


def store(heads, out, stats, summed):
    for h in range(heads):
        rows = slice(h * HEAD, (h + 1) * HEAD)
        out[rows, :] = (summed(h, rows) * stats[h : h + 1, :]).astype(jnp.bfloat16)
    end = heads * HEAD
    rest = stats[8:16, :]
    pieces = []
    for part in range(PARTS):
        piece = rest.astype(jnp.bfloat16).astype(jnp.float32)
        rest = rest - piece
        pieces.append(piece[0:heads])
    pieces.append(jnp.zeros((SPARE - PARTS * heads, rest.shape[1]), jnp.float32))
    out[end : end + SPARE, :] = jnp.concatenate(pieces, axis=0).astype(jnp.bfloat16)


def early_kernel(heads, side, near_weights, far_weights, v, v_near, out):
    def body(weights):
        for h in range(heads):
            out[h * HEAD : (h + 1) * HEAD, :] = weighted(h, weights, v, 0) + weighted(h, weights, v_near, 1)

    by_side(side, body, (near_weights,), (far_weights,))


def finish_kernel(heads, side, near_weights, near_stats, far_weights, far_stats, early, v_far, out):
    def body(weights, stats):
        store(heads, out, stats, lambda h, rows: early[rows, :] + weighted(h, weights, v_far, 2))

    by_side(side, body, (near_weights, near_stats), (far_weights, far_stats))


def visitors_kernel(
    heads, side, near_weights, near_stats, far_weights, far_stats, v, v_near, v_far, out
):
    def body(weights, stats):
        store(
            heads, out, stats,
            lambda h, rows: sum(weighted(h, weights, x, j) for j, x in enumerate((v, v_near, v_far))),
        )

    by_side(side, body, (near_weights, near_stats), (far_weights, far_stats))


def home_kernel(heads, weights, stats, v, v_near, v_far, out):
    for h in range(heads):
        summed = sum(weighted(h, weights, x, j) for j, x in enumerate((v, v_near, v_far)))
        out[h * HEAD : (h + 1) * HEAD, :] = summed * stats[h : h + 1, :]


def level_of(ref, heads):
    spare = ref[heads * HEAD : heads * HEAD + SPARE, :].astype(jnp.float32)
    return spare[0:heads] + spare[heads : 2 * heads] + spare[2 * heads : 3 * heads]


def shares(levels):
    top = functools.reduce(jnp.maximum, levels)
    parts = [jnp.exp2(level - top) for level in levels]
    scale = 1.0 / functools.reduce(jnp.add, parts)
    return [part * scale for part in parts]


def merge_kernel(heads, own, stats, near, out, level_out):
    levels = [stats[8 : 8 + heads, :], level_of(near, heads)]
    top = jnp.maximum(levels[0], levels[1])
    parts = [jnp.exp2(level - top) for level in levels]
    scale = 1.0 / (parts[0] + parts[1])
    level_out[...] = jnp.zeros(level_out.shape, jnp.float32)
    level_out[0:heads, :] = top + jnp.log2(parts[0] + parts[1])
    parts = [part * scale for part in parts]
    for h in range(heads):
        rows = slice(h * HEAD, (h + 1) * HEAD)
        result = own[rows, :] * parts[0][h : h + 1]
        out[rows, :] = result + near[rows, :].astype(jnp.float32) * parts[1][h : h + 1]


def combine_kernel(heads, merged, level, other, out, block, sems):
    parts = shares([level[0:heads, :], level_of(other, heads)])
    rows = block.shape[0]
    half = rows // 2
    copies = []
    for i in range(2):
        lanes = slice(i * half, (i + 1) * half)
        for h in range(heads):
            features = slice(h * HEAD, (h + 1) * HEAD)
            result = merged[features, lanes] * parts[0][h : h + 1, lanes]
            result = result + other[features, lanes].astype(jnp.float32) * parts[1][h : h + 1, lanes]
            block[lanes, features] = result.astype(jnp.bfloat16).T
        copy = pltpu.make_async_copy(block.at[lanes], out.at[lanes], sems.at[i])
        copy.start()
        copies.append(copy)
    for copy in copies:
        copy.wait()


def tile_bias(tile_coords, windows, per_device, gate):
    space_count, tm_count = lax.axis_size("space"), lax.axis_size("tm")
    s, t = lax.axis_index("space"), lax.axis_index("tm")

    def tiles(column, slab):
        device = column * tm_count + slab
        return lax.dynamic_slice_in_dim(tile_coords, device * per_device, per_device, 1)

    slabs = [t, partner(t, NEAR, tm_count), partner(t, FAR, tm_count)]
    columns = [s, partner(s, NEAR, space_count), partner(s, FAR, space_count)]
    key_tiles = jnp.concatenate([tiles(s, slab) for slab in slabs], axis=1)
    queries = jnp.stack([tiles(column, t) for column in columns], axis=1)
    key_tiles, queries, _ = lax.optimization_barrier((key_tiles, queries, gate))
    queries = jnp.repeat(queries, TILE, axis=2)
    gap = jnp.abs(key_tiles[:, None, :, None] - queries[:, :, None, :])
    allowed = jnp.all(gap[:, :, None] <= windows[:, None, :, None, None], axis=0)
    bias = jnp.where(allowed, 0.0, MASKED).astype(jnp.float32)
    return [bias[i].reshape(-1, bias.shape[-1]) for i in range(3)]


def shards(query, key, value, tile_coords, windows):
    heads = windows.shape[1]
    rows = query.shape[0]
    width = heads * HEAD
    f32, bf16 = jnp.float32, jnp.bfloat16
    pair = 2 * rows * HEAD * rows

    k_near = exchange(key, "tm", NEAR)
    k_far = swap_slabs(key)
    mark = call(mark_kernel, jax.ShapeDtypeStruct((8, HEAD), f32), 0)
    sent = after(query, mark)
    q_near = exchange(query, "space", NEAR)
    q_far = exchange(sent, "space", FAR)
    v_near = exchange(value, "tm", NEAR)
    v_far = swap_slabs(after(value, k_near))
    bias = tile_bias(after(tile_coords, k_far), windows, rows // TILE, k_near)

    def weigh(kernel, q, table):
        return call(
            kernel,
            (
                jax.ShapeDtypeStruct((heads, 3 * rows, rows), bf16),
                jax.ShapeDtypeStruct((16, rows), f32),
            ),
            heads * 3 * pair, k_far, k_near, q, key, table,
            exps=heads * 3 * rows * rows,
        )

    always = functools.partial(weigh_kernel, heads)
    near_weights, near_stats = weigh(always, q_near, bias[1])
    odd_weights, odd_stats = weigh(
        functools.partial(weigh_if_kernel, heads, 1), q_far, after(bias[2], near_stats)
    )
    back = jax.ShapeDtypeStruct((width + SPARE, rows), bf16)
    early = call(
        functools.partial(early_kernel, heads, 0), jax.ShapeDtypeStruct((width, rows), f32), 0,
        near_weights, odd_weights, value, v_near,
    )
    to_next = call(
        functools.partial(finish_kernel, heads, 0), back, 0,
        near_weights, near_stats, odd_weights, odd_stats, early, v_far,
    )
    even_weights, even_stats = weigh(
        functools.partial(weigh_if_kernel, heads, 0), q_far, after(bias[2], to_next)
    )
    to_last = call(
        functools.partial(visitors_kernel, heads, 1), back, 0,
        near_weights, near_stats, even_weights, even_stats, value, v_near, v_far,
    )
    own_weights, own_stats = weigh(always, query, after(bias[0], to_last))
    from_last = shift(to_next, "space", 1)
    from_next = shift(to_last, "space", -1)
    own = call(
        functools.partial(home_kernel, heads), jax.ShapeDtypeStruct((width, rows), f32),
        heads * 3 * pair, own_weights, own_stats, value, v_near, v_far,
    )
    merged, level = call(
        functools.partial(merge_kernel, heads),
        (jax.ShapeDtypeStruct((width, rows), f32), jax.ShapeDtypeStruct((8, rows), f32)), 0,
        own, own_stats, from_last,
    )
    return pl.pallas_call(
        functools.partial(combine_kernel, heads),
        out_shape=jax.ShapeDtypeStruct((rows, width), bf16),
        out_specs=pl.BlockSpec(memory_space=pl.ANY),
        scratch_shapes=[pltpu.VMEM((rows, width), bf16), pltpu.SemaphoreType.DMA((2,))],
        compiler_params=pltpu.CompilerParams(vmem_limit_bytes=40 * 1024 * 1024),
        cost_estimate=pl.CostEstimate(flops=0, bytes_accessed=1024, transcendentals=0),
    )(merged, level, from_next)


def solution(mesh):
    placed = (
        P(("space", "tm"), "head"),
        P(("space", "tm"), "head"),
        P(("space", "tm"), "head"),
        P(),
        P(None, "head"),
    )
    return jax.shard_map(
        shards, mesh=mesh, in_specs=placed, out_specs=P(("space", "tm"), "head"), check_vma=False
    )
```

```python
import functools

import jax
import jax.numpy as jnp
from jax import lax
from jax.experimental import pallas as pl
from jax.experimental.pallas import tpu as pltpu
from jax.sharding import PartitionSpec as P

TILE = 64
HEAD = 128
MASKED = -1e30
FLOOR = -1e29
FACTOR = 1.4426950408889634 * HEAD**-0.5
PARTS = 3
SPARE = 16
NEAR, FAR = 0, 1


def partner(index, side, count):
    step = 1 - 2 * (index % 2)
    return (index + (step if side == NEAR else -step)) % count


def exchange(block, axis, side):
    count = lax.axis_size(axis)
    return lax.ppermute(block, axis, [(i, partner(i, side, count)) for i in range(count)])


def shift(block, axis, distance):
    count = lax.axis_size(axis)
    return lax.ppermute(block, axis, [(i, (i + distance) % count) for i in range(count)])


def swap_slabs(block):
    heads, slabs = lax.axis_size("head"), lax.axis_size("tm")
    pairs = []
    for head in range(heads):
        for slab in range(slabs):
            if 0 < slab < slabs - 1:
                there = head * slabs + partner(slab, FAR, slabs)
            else:
                there = partner(head, NEAR, heads) * slabs + slab
            pairs.append((head * slabs + slab, there))
    return lax.ppermute(block, ("head", "tm"), pairs)


def after(block, other):
    return lax.optimization_barrier((block, other))[0]


def call(kernel, out_shape, flops, *operands, exps=0, moved=1 << 20):
    return pl.pallas_call(
        kernel,
        out_shape=out_shape,
        compiler_params=pltpu.CompilerParams(vmem_limit_bytes=40 * 1024 * 1024),
        cost_estimate=pl.CostEstimate(flops=0, bytes_accessed=1024, transcendentals=0),
    )(*operands)


def mark_kernel(out):
    out[...] = jnp.zeros(out.shape, out.dtype)


def weigh_if_kernel(heads, parity, *refs):
    pl.when(lax.axis_index("space") % 2 == parity)(lambda: weigh_kernel(heads, *refs))


def weigh_kernel(heads, key_far, key_near, q, key, bias, weights_out, stats_out):
    stats_out[...] = jnp.zeros(stats_out.shape, jnp.float32)
    tiles = key.shape[0] // TILE
    for h in range(heads):
        lanes = slice(h * HEAD, (h + 1) * HEAD)
        blocks, peak = [], None
        for j, keys in enumerate((key, key_near, key_far)):
            raw = lax.dot_general(
                keys[:, lanes], q[:, lanes], (((1,), (1,)), ((), ())),
                preferred_element_type=jnp.float32,
            )
            for i in range(tiles):
                row = (h * 3 + j) * tiles + i
                block = raw[i * TILE : (i + 1) * TILE] + bias[row : row + 1, :]
                blocks.append(block)
                peak = block if peak is None else jnp.maximum(peak, block)
        peak = jnp.maximum(jnp.max(peak, axis=0, keepdims=True), FLOOR)
        total = None
        for i, block in enumerate(blocks):
            weights = jnp.exp2((block - peak) * FACTOR)
            weights_out[h, i * TILE : (i + 1) * TILE, :] = weights.astype(jnp.bfloat16)
            total = weights if total is None else total + weights
        total = jnp.maximum(jnp.sum(total, axis=0, keepdims=True), 0.5)
        stats_out[h : h + 1, :] = 1.0 / total
        stats_out[8 + h : 9 + h, :] = peak * FACTOR + jnp.log2(total)


def weighted(h, weights, value, j):
    lanes = slice(h * HEAD, (h + 1) * HEAD)
    width = value.shape[0]
    return lax.dot_general(
        value[:, lanes], weights[h, j * width : (j + 1) * width, :],
        (((0,), (0,)), ((), ())), preferred_element_type=jnp.float32,
    )


def by_side(side, body, near, far):
    odd = lax.axis_index("space") % 2
    pl.when(odd == side)(lambda: body(*near))
    pl.when(odd != side)(lambda: body(*far))


def store(heads, out, stats, summed):
    for h in range(heads):
        rows = slice(h * HEAD, (h + 1) * HEAD)
        out[rows, :] = (summed(h, rows) * stats[h : h + 1, :]).astype(jnp.bfloat16)
    end = heads * HEAD
    rest = stats[8:16, :]
    pieces = []
    for part in range(PARTS):
        piece = rest.astype(jnp.bfloat16).astype(jnp.float32)
        rest = rest - piece
        pieces.append(piece[0:heads])
    pieces.append(jnp.zeros((SPARE - PARTS * heads, rest.shape[1]), jnp.float32))
    out[end : end + SPARE, :] = jnp.concatenate(pieces, axis=0).astype(jnp.bfloat16)


def early_kernel(heads, side, near_weights, far_weights, v, v_far, out):
    def body(weights):
        for h in range(heads):
            out[h * HEAD : (h + 1) * HEAD, :] = weighted(h, weights, v, 0) + weighted(h, weights, v_far, 2)

    by_side(side, body, (near_weights,), (far_weights,))


def finish_kernel(heads, side, near_weights, near_stats, far_weights, far_stats, early, v_near, out):
    def body(weights, stats):
        store(heads, out, stats, lambda h, rows: early[rows, :] + weighted(h, weights, v_near, 1))

    by_side(side, body, (near_weights, near_stats), (far_weights, far_stats))


def visitors_kernel(
    heads, side, near_weights, near_stats, far_weights, far_stats, v, v_near, v_far, out
):
    def body(weights, stats):
        store(
            heads, out, stats,
            lambda h, rows: sum(weighted(h, weights, x, j) for j, x in enumerate((v, v_near, v_far))),
        )

    by_side(side, body, (near_weights, near_stats), (far_weights, far_stats))


def home_kernel(heads, weights, stats, v, v_near, v_far, out):
    for h in range(heads):
        summed = sum(weighted(h, weights, x, j) for j, x in enumerate((v, v_near, v_far)))
        out[h * HEAD : (h + 1) * HEAD, :] = summed * stats[h : h + 1, :]


def level_of(ref, heads):
    spare = ref[heads * HEAD : heads * HEAD + SPARE, :].astype(jnp.float32)
    return spare[0:heads] + spare[heads : 2 * heads] + spare[2 * heads : 3 * heads]


def shares(levels):
    top = functools.reduce(jnp.maximum, levels)
    parts = [jnp.exp2(level - top) for level in levels]
    scale = 1.0 / functools.reduce(jnp.add, parts)
    return [part * scale for part in parts]


def combine_kernel(heads, own, stats, last, other, out, block, sems):
    parts = shares([stats[8 : 8 + heads, :], level_of(last, heads), level_of(other, heads)])
    rows = block.shape[0]
    half = rows // 2
    copies = []
    for i in range(2):
        lanes = slice(i * half, (i + 1) * half)
        for h in range(heads):
            features = slice(h * HEAD, (h + 1) * HEAD)
            result = own[features, lanes] * parts[0][h : h + 1, lanes]
            for part, ref in zip(parts[1:], (last, other)):
                result = result + ref[features, lanes].astype(jnp.float32) * part[h : h + 1, lanes]
            block[lanes, features] = result.astype(jnp.bfloat16).T
        copy = pltpu.make_async_copy(block.at[lanes], out.at[lanes], sems.at[i])
        copy.start()
        copies.append(copy)
    for copy in copies:
        copy.wait()


def tile_bias(tile_coords, windows, per_device, gate):
    space_count, tm_count = lax.axis_size("space"), lax.axis_size("tm")
    s, t = lax.axis_index("space"), lax.axis_index("tm")

    def tiles(column, slab):
        device = column * tm_count + slab
        return lax.dynamic_slice_in_dim(tile_coords, device * per_device, per_device, 1)

    slabs = [t, partner(t, NEAR, tm_count), partner(t, FAR, tm_count)]
    columns = [s, partner(s, NEAR, space_count), partner(s, FAR, space_count)]
    key_tiles = jnp.concatenate([tiles(s, slab) for slab in slabs], axis=1)
    queries = jnp.stack([tiles(column, t) for column in columns], axis=1)
    key_tiles, queries, _ = lax.optimization_barrier((key_tiles, queries, gate))
    queries = jnp.repeat(queries, TILE, axis=2)
    gap = jnp.abs(key_tiles[:, None, :, None] - queries[:, :, None, :])
    allowed = jnp.all(gap[:, :, None] <= windows[:, None, :, None, None], axis=0)
    bias = jnp.where(allowed, 0.0, MASKED).astype(jnp.float32)
    return [bias[i].reshape(-1, bias.shape[-1]) for i in range(3)]


def shards(query, key, value, tile_coords, windows):
    heads = windows.shape[1]
    rows = query.shape[0]
    width = heads * HEAD
    f32, bf16 = jnp.float32, jnp.bfloat16
    pair = 2 * rows * HEAD * rows

    k_near = exchange(key, "tm", NEAR)
    k_far = swap_slabs(key)
    mark = call(mark_kernel, jax.ShapeDtypeStruct((8, HEAD), f32), 0)
    sent = after(query, mark)
    q_near = exchange(query, "space", NEAR)
    q_far = exchange(sent, "space", FAR)
    v_far = swap_slabs(value)
    v_near = exchange(after(value, k_near), "tm", NEAR)
    bias = tile_bias(after(tile_coords, k_far), windows, rows // TILE, k_near)

    def weigh(kernel, q, table):
        return call(
            kernel,
            (
                jax.ShapeDtypeStruct((heads, 3 * rows, rows), bf16),
                jax.ShapeDtypeStruct((16, rows), f32),
            ),
            heads * 3 * pair, k_far, k_near, q, key, table,
            exps=heads * 3 * rows * rows,
        )

    always = functools.partial(weigh_kernel, heads)
    near_weights, near_stats = weigh(always, q_near, bias[1])
    odd_weights, odd_stats = weigh(
        functools.partial(weigh_if_kernel, heads, 1), q_far, after(bias[2], near_stats)
    )
    back = jax.ShapeDtypeStruct((width + SPARE, rows), bf16)
    early = call(
        functools.partial(early_kernel, heads, 0), jax.ShapeDtypeStruct((width, rows), f32), 0,
        near_weights, odd_weights, value, v_far,
    )
    to_next = call(
        functools.partial(finish_kernel, heads, 0), back, 0,
        near_weights, near_stats, odd_weights, odd_stats, early, v_near,
    )
    even_weights, even_stats = weigh(
        functools.partial(weigh_if_kernel, heads, 0), q_far, after(bias[2], to_next)
    )
    to_last = call(
        functools.partial(visitors_kernel, heads, 1), back, 0,
        near_weights, near_stats, even_weights, even_stats, value, v_near, v_far,
    )
    own_weights, own_stats = weigh(always, query, after(bias[0], to_last))
    from_last = shift(to_next, "space", 1)
    from_next = shift(to_last, "space", -1)
    own = call(
        functools.partial(home_kernel, heads), jax.ShapeDtypeStruct((width, rows), f32),
        heads * 3 * pair, own_weights, own_stats, value, v_near, v_far,
    )
    return pl.pallas_call(
        functools.partial(combine_kernel, heads),
        out_shape=jax.ShapeDtypeStruct((rows, width), bf16),
        out_specs=pl.BlockSpec(memory_space=pl.ANY),
        scratch_shapes=[pltpu.VMEM((rows, width), bf16), pltpu.SemaphoreType.DMA((2,))],
        compiler_params=pltpu.CompilerParams(vmem_limit_bytes=40 * 1024 * 1024),
        cost_estimate=pl.CostEstimate(flops=0, bytes_accessed=1024, transcendentals=0),
    )(own, own_stats, from_last, from_next)


def solution(mesh):
    placed = (
        P(("space", "tm"), "head"),
        P(("space", "tm"), "head"),
        P(("space", "tm"), "head"),
        P(),
        P(None, "head"),
    )
    return jax.shard_map(
        shards, mesh=mesh, in_specs=placed, out_specs=P(("space", "tm"), "head"), check_vma=False
    )
```

```python
import functools

import jax
import jax.numpy as jnp
from jax import lax
from jax.experimental import pallas as pl
from jax.experimental.pallas import tpu as pltpu
from jax.sharding import PartitionSpec as P

TILE = 64
HEAD = 128
MASKED = -1e30
FLOOR = -1e29
FACTOR = 1.4426950408889634 * HEAD**-0.5
PARTS = 3
SPARE = 16
NEAR, FAR = 0, 1


def partner(index, side, count):
    step = 1 - 2 * (index % 2)
    return (index + (step if side == NEAR else -step)) % count


def exchange(block, axis, side):
    count = lax.axis_size(axis)
    return lax.ppermute(block, axis, [(i, partner(i, side, count)) for i in range(count)])


def shift(block, axis, distance):
    count = lax.axis_size(axis)
    return lax.ppermute(block, axis, [(i, (i + distance) % count) for i in range(count)])


def swap_slabs(block):
    heads, slabs = lax.axis_size("head"), lax.axis_size("tm")
    pairs = []
    for head in range(heads):
        for slab in range(slabs):
            if 0 < slab < slabs - 1:
                there = head * slabs + partner(slab, FAR, slabs)
            else:
                there = partner(head, NEAR, heads) * slabs + slab
            pairs.append((head * slabs + slab, there))
    return lax.ppermute(block, ("head", "tm"), pairs)


def after(block, other):
    return lax.optimization_barrier((block, other))[0]


def call(kernel, out_shape, flops, *operands, exps=0, moved=1 << 20):
    return pl.pallas_call(
        kernel,
        out_shape=out_shape,
        compiler_params=pltpu.CompilerParams(vmem_limit_bytes=40 * 1024 * 1024),
        cost_estimate=pl.CostEstimate(flops=0, bytes_accessed=1024, transcendentals=0),
    )(*operands)


def mark_kernel(out):
    out[...] = jnp.zeros(out.shape, out.dtype)


def weigh_if_kernel(heads, parity, *refs):
    pl.when(lax.axis_index("space") % 2 == parity)(lambda: weigh_kernel(heads, *refs))


def weigh_kernel(heads, key_far, key_near, q, key, bias, weights_out, stats_out):
    stats_out[...] = jnp.zeros(stats_out.shape, jnp.float32)
    tiles = key.shape[0] // TILE
    for h in range(heads):
        lanes = slice(h * HEAD, (h + 1) * HEAD)
        blocks, peak = [], None
        for j, keys in enumerate((key, key_near, key_far)):
            raw = lax.dot_general(
                keys[:, lanes], q[:, lanes], (((1,), (1,)), ((), ())),
                preferred_element_type=jnp.float32,
            )
            for i in range(tiles):
                row = (h * 3 + j) * tiles + i
                block = raw[i * TILE : (i + 1) * TILE] + bias[row : row + 1, :]
                blocks.append(block)
                peak = block if peak is None else jnp.maximum(peak, block)
        peak = jnp.maximum(jnp.max(peak, axis=0, keepdims=True), FLOOR)
        total = None
        for i, block in enumerate(blocks):
            weights = jnp.exp2((block - peak) * FACTOR)
            weights_out[h, i * TILE : (i + 1) * TILE, :] = weights.astype(jnp.bfloat16)
            total = weights if total is None else total + weights
        total = jnp.maximum(jnp.sum(total, axis=0, keepdims=True), 0.5)
        stats_out[h : h + 1, :] = 1.0 / total
        stats_out[8 + h : 9 + h, :] = peak * FACTOR + jnp.log2(total)


def weighted(h, weights, value, j):
    lanes = slice(h * HEAD, (h + 1) * HEAD)
    width = value.shape[0]
    return lax.dot_general(
        value[:, lanes], weights[h, j * width : (j + 1) * width, :],
        (((0,), (0,)), ((), ())), preferred_element_type=jnp.float32,
    )


def by_side(side, body, near, far):
    odd = lax.axis_index("space") % 2
    pl.when(odd == side)(lambda: body(*near))
    pl.when(odd != side)(lambda: body(*far))


def store(heads, out, stats, summed):
    for h in range(heads):
        rows = slice(h * HEAD, (h + 1) * HEAD)
        out[rows, :] = (summed(h, rows) * stats[h : h + 1, :]).astype(jnp.bfloat16)
    end = heads * HEAD
    rest = stats[8:16, :]
    pieces = []
    for part in range(PARTS):
        piece = rest.astype(jnp.bfloat16).astype(jnp.float32)
        rest = rest - piece
        pieces.append(piece[0:heads])
    pieces.append(jnp.zeros((SPARE - PARTS * heads, rest.shape[1]), jnp.float32))
    out[end : end + SPARE, :] = jnp.concatenate(pieces, axis=0).astype(jnp.bfloat16)


def early_kernel(heads, side, near_weights, far_weights, v, v_near, out):
    def body(weights):
        for h in range(heads):
            out[h * HEAD : (h + 1) * HEAD, :] = weighted(h, weights, v, 0) + weighted(h, weights, v_near, 1)

    by_side(side, body, (near_weights,), (far_weights,))


def finish_kernel(heads, side, near_weights, near_stats, far_weights, far_stats, early, v_far, out):
    def body(weights, stats):
        store(heads, out, stats, lambda h, rows: early[rows, :] + weighted(h, weights, v_far, 2))

    by_side(side, body, (near_weights, near_stats), (far_weights, far_stats))


def visitors_kernel(
    heads, side, near_weights, near_stats, far_weights, far_stats, v, v_near, v_far, out
):
    def body(weights, stats):
        store(
            heads, out, stats,
            lambda h, rows: sum(weighted(h, weights, x, j) for j, x in enumerate((v, v_near, v_far))),
        )

    by_side(side, body, (near_weights, near_stats), (far_weights, far_stats))


def home_kernel(heads, weights, stats, v, v_near, v_far, out):
    for h in range(heads):
        summed = sum(weighted(h, weights, x, j) for j, x in enumerate((v, v_near, v_far)))
        out[h * HEAD : (h + 1) * HEAD, :] = summed * stats[h : h + 1, :]


def level_of(ref, heads):
    spare = ref[heads * HEAD : heads * HEAD + SPARE, :].astype(jnp.float32)
    return spare[0:heads] + spare[heads : 2 * heads] + spare[2 * heads : 3 * heads]


def shares(levels):
    top = functools.reduce(jnp.maximum, levels)
    parts = [jnp.exp2(level - top) for level in levels]
    scale = 1.0 / functools.reduce(jnp.add, parts)
    return [part * scale for part in parts]


def combine_kernel(heads, own, stats, last, other, out, block, sems):
    parts = shares([stats[8 : 8 + heads, :], level_of(last, heads), level_of(other, heads)])
    rows = block.shape[0]
    half = rows // 2
    copies = []
    for i in range(2):
        lanes = slice(i * half, (i + 1) * half)
        for h in range(heads):
            features = slice(h * HEAD, (h + 1) * HEAD)
            result = own[features, lanes] * parts[0][h : h + 1, lanes]
            for part, ref in zip(parts[1:], (last, other)):
                result = result + ref[features, lanes].astype(jnp.float32) * part[h : h + 1, lanes]
            block[lanes, features] = result.astype(jnp.bfloat16).T
        copy = pltpu.make_async_copy(block.at[lanes], out.at[lanes], sems.at[i])
        copy.start()
        copies.append(copy)
    for copy in copies:
        copy.wait()


def tile_bias(tile_coords, windows, per_device, gate):
    space_count, tm_count = lax.axis_size("space"), lax.axis_size("tm")
    s, t = lax.axis_index("space"), lax.axis_index("tm")

    def tiles(column, slab):
        device = column * tm_count + slab
        return lax.dynamic_slice_in_dim(tile_coords, device * per_device, per_device, 1)

    slabs = [t, partner(t, NEAR, tm_count), partner(t, FAR, tm_count)]
    columns = [s, partner(s, NEAR, space_count), partner(s, FAR, space_count)]
    key_tiles = jnp.concatenate([tiles(s, slab) for slab in slabs], axis=1)
    queries = jnp.stack([tiles(column, t) for column in columns], axis=1)
    key_tiles, queries, _ = lax.optimization_barrier((key_tiles, queries, gate))
    queries = jnp.repeat(queries, TILE, axis=2)
    gap = jnp.abs(key_tiles[:, None, :, None] - queries[:, :, None, :])
    allowed = jnp.all(gap[:, :, None] <= windows[:, None, :, None, None], axis=0)
    bias = jnp.where(allowed, 0.0, MASKED).astype(jnp.float32)
    return [bias[i].reshape(-1, bias.shape[-1]) for i in range(3)]


def shards(query, key, value, tile_coords, windows):
    heads = windows.shape[1]
    rows = query.shape[0]
    width = heads * HEAD
    f32, bf16 = jnp.float32, jnp.bfloat16
    pair = 2 * rows * HEAD * rows

    k_near = exchange(key, "tm", NEAR)
    k_far = swap_slabs(key)
    mark = call(mark_kernel, jax.ShapeDtypeStruct((8, HEAD), f32), 0)
    sent = after(query, mark)
    q_near = exchange(query, "space", NEAR)
    q_far = exchange(sent, "space", FAR)
    v_near = exchange(value, "tm", NEAR)
    v_far = swap_slabs(after(value, k_near))
    bias = tile_bias(after(tile_coords, k_far), windows, rows // TILE, k_near)

    def weigh(kernel, q, table):
        return call(
            kernel,
            (
                jax.ShapeDtypeStruct((heads, 3 * rows, rows), bf16),
                jax.ShapeDtypeStruct((16, rows), f32),
            ),
            heads * 3 * pair, k_far, k_near, q, key, table,
            exps=heads * 3 * rows * rows,
        )

    always = functools.partial(weigh_kernel, heads)
    near_weights, near_stats = weigh(always, q_near, bias[1])
    odd_weights, odd_stats = weigh(
        functools.partial(weigh_if_kernel, heads, 1), q_far, after(bias[2], near_stats)
    )
    back = jax.ShapeDtypeStruct((width + SPARE, rows), bf16)
    early = call(
        functools.partial(early_kernel, heads, 0), jax.ShapeDtypeStruct((width, rows), f32), 0,
        near_weights, odd_weights, value, v_near,
    )
    to_next = call(
        functools.partial(finish_kernel, heads, 0), back, 0,
        near_weights, near_stats, odd_weights, odd_stats, early, v_far,
    )
    even_weights, even_stats = weigh(
        functools.partial(weigh_if_kernel, heads, 0), q_far, after(bias[2], to_next)
    )
    to_last = call(
        functools.partial(visitors_kernel, heads, 1), back, 0,
        near_weights, near_stats, even_weights, even_stats, value, v_near, v_far,
    )
    own_weights, own_stats = weigh(always, query, after(bias[0], to_last))
    from_last = shift(to_next, "space", 1)
    from_next = shift(to_last, "space", -1)
    own = call(
        functools.partial(home_kernel, heads), jax.ShapeDtypeStruct((width, rows), f32),
        heads * 3 * pair, own_weights, own_stats, value, v_near, v_far,
    )
    return pl.pallas_call(
        functools.partial(combine_kernel, heads),
        out_shape=jax.ShapeDtypeStruct((rows, width), bf16),
        out_specs=pl.BlockSpec(memory_space=pl.ANY),
        scratch_shapes=[pltpu.VMEM((rows, width), bf16), pltpu.SemaphoreType.DMA((2,))],
        compiler_params=pltpu.CompilerParams(vmem_limit_bytes=40 * 1024 * 1024),
        cost_estimate=pl.CostEstimate(flops=0, bytes_accessed=1024, transcendentals=0),
    )(own, own_stats, from_last, from_next)


def solution(mesh):
    placed = (
        P(("space", "tm"), "head"),
        P(("space", "tm"), "head"),
        P(("space", "tm"), "head"),
        P(),
        P(None, "head"),
    )
    return jax.shard_map(
        shards, mesh=mesh, in_specs=placed, out_specs=P(("space", "tm"), "head"), check_vma=False
    )
```
